128 devices in a mesh: shot: 8 (over x, y_hi), slab: 16 (over y_lo, z, core).
Axes of the slice: x: 4, y: 4 (y_hi: 2, y_lo: 2; y = y_hi * 2 + y_lo), z: 4, core: 2. Of those that a mesh axis runs over, the one named last changes fastest.
Arguments:
- velocity: bfloat16 [192, 128, 256], P('shot', 'slab'), may hold values from 0.099609375 to 0.29882812
- epsilon: bfloat16 [192, 128, 256], P('shot', 'slab'), may hold values from 0.19921875 to 0.3984375
- delta: bfloat16 [192, 128, 256], P('shot', 'slab'), may hold values from 0 to 0.19921875
- tilt: bfloat16 [192, 128, 256], P('shot', 'slab'), may hold values from -3.140625 to 3.140625
- azimuth: bfloat16 [192, 128, 256], P('shot', 'slab'), may hold values from -3.140625 to 3.140625
- offsets: int32 [8, 2], replicated, may hold values from 0 to 128, as said below
- sources: int32 [8], P('shot'), may hold values from 0 to 1572863
- traces: float32 [8, 12], P('shot'), may hold values from -60 to 60
- adjoint_state: float32 [4, 8, 192, 64, 128], P(None, 'shot', 'slab'), may hold values from -6 to 6
- snapshots: bfloat16 [12, 2, 8, 192, 64, 128], P(None, None, 'shot', 'slab'), may hold values from -1.1953125 to 1.1953125
Outputs:
- gradients: float32 [5, 192, 128, 256], P(None, 'shot', 'slab')
- adjoint_final: float32 [2, 8, 192, 64, 128], P(None, 'shot', 'slab')
The draws below stay inside these ranges and needn't reach their ends.
Inputs may be any that keep to these rules, and one draw needn't show every extreme that they name: offsets[s] = (first lateral, second lateral) earth cell of the aperture's first cell; the first is at most 64, the second at most 128. sources[s] names the cell z * 64 * 128 + x * 128 + y of shot s's aperture.
All inputs are finite; a program needn't handle non-finite values.
Results may differ from the reference program's by a relative error of at most 0.0008.
Values may be sent and summed in bfloat16 or wider, within the bound.
A program may use at most 192 MiB of HBM per device.

```python
import math
import jax
import jax.numpy as jnp
from jax import lax

AX = 64
AY = 128
STEPS = 12
SHOTS = 8
GZ = 192
GX = 128
GY = 256


def draw_offsets(key, part):
    key = jax.random.fold_in(key, 11)
    key_columns, key_lanes, key_ordering = jax.random.split(key, 3)
    column_starts = jax.random.randint(key_columns, (SHOTS,), 0, GX - AX + 1)
    lane_starts = jax.random.randint(key_lanes, (SHOTS,), 0, GY - AY + 1)
    ordering = jax.random.permutation(key_ordering, SHOTS)
    lane_starts = lane_starts.at[ordering[0]].set(GY - AY)
    column_starts = column_starts.at[ordering[1]].set(0)
    return jnp.stack([column_starts, lane_starts], axis=1).astype(jnp.int32)


def plant(result, key, low, largest):
    place = [jax.random.randint(jax.random.fold_in(key, axis), (), 0, length) for axis, length in enumerate(result.shape)]
    longest = result.shape.index(max(result.shape))
    neighbour = place[:longest] + [(place[longest] + 1) % result.shape[longest]] + place[longest + 1:]
    return result.at[tuple(place)].set(low).at[tuple(neighbour)].set(largest)


def steps_of(own_key, dims, cuts, least, high):
    gain, own = 1.0, jax.random.fold_in(own_key, 6)
    for dim, blocks in cuts:
        steps = jnp.exp(jax.random.uniform(jax.random.fold_in(own, dim), (blocks,), jnp.float32, least / len(cuts), high / len(cuts)))
        gain = gain * jnp.repeat(steps, dims[dim] // blocks).reshape([-1 if axis == dim else 1 for axis in range(len(dims))])
    return gain


def gaussian(stream_key, extent, spread, reach, cuts=(), dtype=jnp.bfloat16):
    drawn = spread * jax.random.normal(stream_key, extent, jnp.float32)
    if cuts:
        drawn = drawn * steps_of(stream_key, extent, cuts, -0.22, 0.18)
    return jnp.clip(drawn, -reach, reach).astype(dtype)


def setup_inputs(seed: int = 0) -> dict:
    keys = jax.random.split(jax.random.key(seed), 11)
    velocity = jnp.clip(jnp.exp(math.log(0.29882812) - 1.0986123 * jax.random.uniform(keys[0], (GZ, GX, GY), jnp.float32) ** steps_of(keys[0], (GZ, GX, GY), ((0, 8), (1, 16)), -0.2, 0.2)), 0.099609375, 0.29882812).astype(jnp.bfloat16)
    epsilon = jnp.clip(0.19921875 + 0.19921875 * jax.random.uniform(keys[1], (GZ, GX, GY), jnp.float32) ** steps_of(keys[1], (GZ, GX, GY), ((0, 8), (1, 16)), -0.2, 0.2), 0.19921875, 0.3984375).astype(jnp.bfloat16)
    delta = jnp.clip(0.19921875 * jax.random.uniform(keys[2], (GZ, GX, GY), jnp.float32) ** steps_of(keys[2], (GZ, GX, GY), ((0, 8), (1, 16)), -0.2, 0.2), 0.0, 0.19921875).astype(jnp.bfloat16)
    tilt = jnp.clip(jax.random.uniform(keys[3], (GZ, GX, GY), jnp.float32, -3.140625, 3.140625), -3.140625, 3.140625).astype(jnp.bfloat16)
    azimuth = jnp.clip(jax.random.uniform(keys[4], (GZ, GX, GY), jnp.float32, -3.140625, 3.140625), -3.140625, 3.140625).astype(jnp.bfloat16)
    offsets = draw_offsets(jax.random.fold_in(keys[10], 71), 0)
    sources = plant(jax.random.randint(keys[6], (SHOTS,), 0, GZ * AX * AY), jax.random.fold_in(keys[6], 1), 0, (GZ * AX * AY) - 1).astype(jnp.int32)
    traces = gaussian(keys[7], (SHOTS, STEPS), 10.0, 60.0, ((0, 8),), jnp.float32)
    adjoint_state = gaussian(keys[8], (4, SHOTS, GZ, AX, AY), 1.0, 6.0, ((1, 8), (2, 16)), jnp.float32)
    snapshots = gaussian(keys[9], (STEPS, 2, SHOTS, GZ, AX, AY), 0.2, 1.1953125, ((2, 8), (3, 16)))
    return dict(velocity=velocity, epsilon=epsilon, delta=delta, tilt=tilt, azimuth=azimuth, offsets=offsets, sources=sources, traces=traces, adjoint_state=adjoint_state, snapshots=snapshots)


centred_second = (-205.0 / 72.0, 8.0 / 5.0, -1.0 / 5.0, 8.0 / 315.0, -1.0 / 560.0)
centred_first = (4.0 / 5.0, -1.0 / 5.0, 4.0 / 105.0, -1.0 / 280.0)

def shifted(source_field, along_axis, distance):
    length = source_field.shape[along_axis]
    widths = [(0, 0)] * source_field.ndim
    widths[along_axis] = (4, 4)
    padded = jnp.pad(source_field, widths)
    return lax.slice_in_dim(padded, 4 + distance, 4 + distance + length, axis=along_axis)

def second_along(source_field, along_axis):
    summed = centred_second[0] * source_field
    for distance in range(1, 5):
        summed = summed + centred_second[distance] * (shifted(source_field, along_axis, distance) + shifted(source_field, along_axis, -distance))
    return summed

def first_along(source_field, along_axis):
    summed = centred_first[0] * (shifted(source_field, along_axis, 1) - shifted(source_field, along_axis, -1))
    for distance in range(2, 5):
        summed = summed + centred_first[distance - 1] * (shifted(source_field, along_axis, distance) - shifted(source_field, along_axis, -distance))
    return summed

def rows_second(extended, row_count):
    summed = centred_second[0] * extended[4:4 + row_count]
    for distance in range(1, 5):
        summed = summed + centred_second[distance] * (extended[4 + distance:4 + distance + row_count] + extended[4 - distance:4 - distance + row_count])
    return summed

def rows_first(extended, row_count):
    summed = centred_first[0] * (extended[5:5 + row_count] - extended[3:3 + row_count])
    for distance in range(2, 5):
        summed = summed + centred_first[distance - 1] * (extended[4 + distance:4 + distance + row_count] - extended[4 - distance:4 - distance + row_count])
    return summed

def derivatives(extended):
    row_count = extended.shape[0] - 8
    centre = extended[4:4 + row_count]
    along_x = first_along(extended, 1)
    along_y = first_along(extended, 2)
    return (rows_second(extended, row_count), second_along(centre, 1), second_along(centre, 2), rows_first(along_x, row_count), rows_first(along_y, row_count), first_along(along_x[4:4 + row_count], 2))

def quadratic(first_vector, second_vector, second_parts):
    summed = first_vector[0] * second_vector[0] * second_parts[0] + first_vector[1] * second_vector[1] * second_parts[1]
    summed = summed + first_vector[2] * second_vector[2] * second_parts[2]
    summed = summed + (first_vector[0] * second_vector[1] + first_vector[1] * second_vector[0]) * second_parts[3]
    summed = summed + (first_vector[0] * second_vector[2] + first_vector[2] * second_vector[0]) * second_parts[4]
    return summed + (first_vector[1] * second_vector[2] + first_vector[2] * second_vector[1]) * second_parts[5]

def prepare(parameters):
    wavespeed = parameters[0]
    tilt_sine = jnp.sin(parameters[3])
    tilt_cosine = jnp.cos(parameters[3])
    azimuth_sine = jnp.sin(parameters[4])
    azimuth_cosine = jnp.cos(parameters[4])
    normal = (tilt_cosine, tilt_sine * azimuth_cosine, tilt_sine * azimuth_sine)
    tilted = (-tilt_sine, tilt_cosine * azimuth_cosine, tilt_cosine * azimuth_sine)
    turned = (jnp.zeros_like(wavespeed), -tilt_sine * azimuth_sine, tilt_sine * azimuth_cosine)
    return (wavespeed, wavespeed * wavespeed, 1.0 + 2.0 * parameters[1], jnp.sqrt(1.0 + 2.0 * parameters[2])) + normal + tilted + turned

def advance(primary_ext, coupled_ext, primary_prev, coupled_prev, prepared, first_row, total_rows, amplitude, source):
    factor = prepared[1]
    stretch = prepared[2]
    coupling = prepared[3]
    normal = prepared[4:7]
    tilted = prepared[7:10]
    turned = prepared[10:13]
    row_count = primary_prev.shape[0]
    across = primary_prev.shape[1]
    lane_count = primary_prev.shape[2]
    parts_primary = derivatives(primary_ext)
    parts_coupled = derivatives(coupled_ext)
    axial_primary = quadratic(normal, normal, parts_primary)
    across_primary = parts_primary[0] + parts_primary[1] + parts_primary[2] - axial_primary
    axial_coupled = quadratic(normal, normal, parts_coupled)
    drive_primary = stretch * across_primary + coupling * axial_coupled
    drive_coupled = coupling * across_primary + axial_coupled
    tilt_primary = 2.0 * quadratic(tilted, normal, parts_primary)
    tilt_coupled = 2.0 * quadratic(tilted, normal, parts_coupled)
    turn_primary = 2.0 * quadratic(turned, normal, parts_primary)
    turn_coupled = 2.0 * quadratic(turned, normal, parts_coupled)
    depth_index = first_row + lax.broadcasted_iota(jnp.int32, (row_count, 1, 1), 0)
    column_index = lax.broadcasted_iota(jnp.int32, (1, across, 1), 1)
    lane_index = lax.broadcasted_iota(jnp.int32, (1, 1, lane_count), 2)
    source_depth = source // (across * lane_count)
    source_column = source // lane_count % across
    source_lane = source % lane_count
    at_source = (depth_index == source_depth) & (column_index == source_column) & (lane_index == source_lane)
    inside = (depth_index >= 0) & (depth_index < total_rows)
    centre_primary = primary_ext[4:4 + row_count]
    centre_coupled = coupled_ext[4:4 + row_count]
    primary_next = 2.0 * centre_primary - primary_prev + factor * drive_primary + jnp.where(at_source, factor * amplitude, 0.0)
    coupled_next = 2.0 * centre_coupled - coupled_prev + factor * drive_coupled
    primary_next = jnp.where(inside, primary_next, 0.0)
    coupled_next = jnp.where(inside, coupled_next, 0.0)
    images = (drive_primary, drive_coupled, across_primary, axial_coupled, tilt_primary, tilt_coupled, turn_primary, turn_coupled)
    return (primary_next, coupled_next, images)

def correlate(gradients, images, prepared, forward_primary, forward_coupled):
    wavespeed = prepared[0]
    factor = prepared[1]
    stretch = prepared[2]
    coupling = prepared[3]
    drive_primary, drive_coupled, across_primary, axial_coupled, tilt_primary, tilt_coupled, turn_primary, turn_coupled = images
    increments = jnp.stack([2.0 * wavespeed * (drive_primary * forward_primary + drive_coupled * forward_coupled), 2.0 * factor * across_primary * forward_primary, factor / coupling * (axial_coupled * forward_primary + across_primary * forward_coupled), factor * ((coupling * tilt_coupled - stretch * tilt_primary) * forward_primary + (tilt_coupled - coupling * tilt_primary) * forward_coupled), factor * ((coupling * turn_coupled - stretch * turn_primary) * forward_primary + (turn_coupled - coupling * turn_primary) * forward_coupled)])
    return gradients + increments

def reference(velocity, epsilon, delta, tilt, azimuth, offsets, sources, traces, adjoint_state, snapshots):
    earth_model = jnp.stack([velocity, epsilon, delta, tilt, azimuth])
    states = jnp.moveaxis(adjoint_state, 1, 0)
    frames = jnp.moveaxis(snapshots, 2, 0)

    def one_shot(inputs):
        state, frame, offset, source, amplitudes = inputs
        starts = (jnp.int32(0), jnp.int32(0), offset[0].astype(jnp.int32), offset[1].astype(jnp.int32))
        window = lax.dynamic_slice(earth_model, starts, (5, GZ, AX, AY))
        prepared = prepare(window.astype(jnp.float32))
        gradient_zero = jnp.zeros((5, GZ, AX, AY), jnp.float32)
        widths = ((4, 4), (0, 0), (0, 0))

        def one_step(step_index, carry):
            primary, coupled, primary_prev, coupled_prev, gradients = carry
            primary_next, coupled_next, images = advance(jnp.pad(primary, widths), jnp.pad(coupled, widths), primary_prev, coupled_prev, prepared, 0, GZ, amplitudes[step_index], source)
            gradients = correlate(gradients, images, prepared, frame[step_index, 0].astype(jnp.float32), frame[step_index, 1].astype(jnp.float32))
            return (primary_next, coupled_next, primary, coupled, gradients)
        final = lax.fori_loop(0, STEPS, one_step, (state[0], state[1], state[2], state[3], gradient_zero))
        return (jnp.stack([final[0], final[1]]), final[4])
    finals, shot_gradients = lax.map(one_shot, (states, frames, offsets, sources, traces))

    def add_shot(shot_number, summed):
        offset = offsets[shot_number]
        starts = (jnp.int32(0), jnp.int32(0), offset[0].astype(jnp.int32), offset[1].astype(jnp.int32))
        current = lax.dynamic_slice(summed, starts, (5, GZ, AX, AY))
        return lax.dynamic_update_slice(summed, current + shot_gradients[shot_number], starts)
    gradients = lax.fori_loop(0, SHOTS, add_shot, jnp.zeros((5, GZ, GX, GY), jnp.float32))
    return (gradients, jnp.moveaxis(finals, 0, 1))
```

```python
import functools
import jax
import jax.numpy as jnp
from jax import lax
from jax.sharding import PartitionSpec as P
from jax.experimental import pallas as pl
from jax.experimental.pallas import tpu as pltpu

MESH = pl.DeviceIdType.MESH
F32 = jnp.float32
BF16 = jnp.bfloat16

SECOND = (63.0, -7.875, 1.0, -9.0 / 128.0)
FIRST = (21.0, -5.25, 1.0, -3.0 / 32.0)
UNIT2 = 8.0 / 315.0
UNIT11 = (4.0 / 105.0) ** 2
CENTRE = -7175.0 / 64.0
VMEM_LIMIT = 60 * 1024 * 1024


def second(at):
    total = at(3) + at(-3)
    for k in (1, 2, 4):
        total = total + SECOND[k - 1] * (at(k) + at(-k))
    return total


def first(at):
    total = at(3) - at(-3)
    for k in (1, 2, 4):
        total = total + FIRST[k - 1] * (at(k) - at(-k))
    return total


def sine_cosine(angle):
    u = 0.5 * angle
    w = u * u
    s = 1.0 / 362880.0 - w * (1.0 / 39916800.0)
    for term in (-1.0 / 5040.0, 1.0 / 120.0, -1.0 / 6.0, 1.0):
        s = term + w * s
    s = s * u
    c = -1.0 / 3628800.0 + w * (1.0 / 479001600.0)
    for term in (1.0 / 40320.0, -1.0 / 720.0, 1.0 / 24.0, -0.5, 1.0):
        c = term + w * c
    return 2.0 * s * c, 1.0 - 2.0 * s * s


def where_am_i():
    me_s = lax.axis_index("shot")
    me_b = lax.axis_index("slab")
    half = lax.axis_size("slab") // 2
    return me_s, me_b, half, me_b // half, lax.rem(me_b, half)


def fetch_kernel(v_ref, e_ref, d_ref, t_ref, a_ref, offsets_ref, out_ref,
                 both, sendbuf, psend, precv, send_sem, recv_sem, loc_sem):
    me_s, me_b, half, h, j_me = where_am_i()
    shots = lax.axis_size("shot")
    partner = (me_s, lax.rem(me_b + half, 2 * half))
    target = 2 * me_s + h
    is_self = target == me_b
    not_self = target != me_b
    rows = sendbuf.shape[1] // 5
    src_s, src_h = me_b // 2, lax.rem(me_b, 2)

    barrier = pltpu.get_barrier_semaphore()
    pl.semaphore_signal(barrier, inc=1, device_id=partner, device_id_type=MESH)
    for j in range(half):
        src_b = src_h * half + j

        @pl.when((src_s != me_s) | (src_b != me_b))
        def _():
            pl.semaphore_signal(barrier, inc=1, device_id=(src_s, src_b), device_id_type=MESH)
    pl.semaphore_wait(barrier, 1 + shots - is_self.astype(jnp.int32))

    params = (v_ref, e_ref, d_ref, t_ref, a_ref)
    theirs = pl.ds(pl.multiple_of(rows * (1 - h), 16), rows)
    ours = pl.ds(pl.multiple_of(rows * h, 16), rows)
    swaps = [
        pltpu.make_async_remote_copy(
            src_ref=params[k].at[theirs], dst_ref=both.at[h, k],
            send_sem=psend.at[k], recv_sem=precv.at[k],
            device_id=partner, device_id_type=MESH)
        for k in range(5)
    ]
    for c in swaps:
        c.start()
    for k in range(5):
        both[h, k] = params[k][ours]
    for c in swaps:
        c.wait()

    row_id = lax.broadcasted_iota(jnp.int32, (16, 128), 0)
    residue = j_me * 8 + lax.rem(row_id, 8)
    lane = lax.broadcasted_iota(jnp.int32, (16, 128), 1)

    def outgoing(i):
        s = lax.rem(me_s + i, shots)
        return s, pltpu.make_async_remote_copy(
            src_ref=sendbuf.at[i], dst_ref=out_ref.at[j_me],
            send_sem=send_sem.at[i], recv_sem=recv_sem.at[j_me],
            device_id=(s, target), device_id_type=MESH)

    local = pltpu.make_async_copy(sendbuf.at[0], out_ref.at[j_me], loc_sem)
    for i in range(shots):
        s, copy = outgoing(i)
        upper = residue < offsets_ref[s, 0]
        right = lane < offsets_ref[s, 1]
        for k in range(5):
            @pl.loop(0, rows // 16)
            def _(r):
                at = pl.ds(pl.multiple_of(r * 16, 16), 16)
                lo = both[0, k, at].astype(F32)
                hi = both[1, k, at].astype(F32)
                left_part = jnp.where(upper, hi[:, :128], lo[:, :128])
                right_part = jnp.where(upper, hi[:, 128:], lo[:, 128:])
                sendbuf[i, pl.ds(pl.multiple_of(k * rows + r * 16, 16), 16)] = (
                    jnp.where(right, right_part, left_part).astype(BF16))
        if i == 0:
            @pl.when(not_self)
            def _():
                copy.start()

            @pl.when(is_self)
            def _():
                local.start()
        else:
            copy.start()
    for i in range(shots):
        s, copy = outgoing(i)
        if i == 0:
            @pl.when(not_self)
            def _():
                copy.wait_send()

            @pl.when(is_self)
            def _():
                local.wait()
        else:
            copy.wait_send()
    for j in range(half):
        @pl.when((src_s != me_s) | (src_h * half + j != me_b))
        def _():
            pltpu.make_async_remote_copy(
                src_ref=sendbuf.at[0], dst_ref=out_ref.at[j],
                send_sem=send_sem.at[0], recv_sem=recv_sem.at[j],
                device_id=(src_s, src_h * half + j), device_id_type=MESH).wait_recv()


def return_kernel(g_ref, offsets_ref, out_ref, recv, acc, send_sem, recv_sem, loc_sem, psend, precv):
    me_s, me_b, half, h, j_me = where_am_i()
    shots = lax.axis_size("shot")
    partner = (me_s, lax.rem(me_b + half, 2 * half))
    rows = g_ref.shape[1] // 5
    to_s, to_h = me_b // 2, lax.rem(me_b, 2)
    from_b = 2 * me_s + h
    is_self = from_b == me_b

    barrier = pltpu.get_barrier_semaphore()
    pl.semaphore_signal(barrier, inc=1, device_id=partner, device_id_type=MESH)
    for i in range(shots):
        s = lax.rem(me_s + i, shots)
        if i == 0:
            @pl.when(from_b != me_b)
            def _():
                pl.semaphore_signal(barrier, inc=1, device_id=(s, from_b), device_id_type=MESH)
        else:
            pl.semaphore_signal(barrier, inc=1, device_id=(s, from_b), device_id_type=MESH)
    pl.semaphore_wait(barrier, 1 + half - is_self.astype(jnp.int32))

    def outgoing(i):
        j = lax.rem(j_me + i, half)
        to_b = to_h * half + j
        mine = (to_s == me_s) & (to_b == me_b)
        return mine, j, pltpu.make_async_remote_copy(
            src_ref=g_ref.at[j], dst_ref=recv.at[me_s],
            send_sem=send_sem.at[i], recv_sem=recv_sem.at[me_s],
            device_id=(to_s, to_b), device_id_type=MESH)

    local = pltpu.make_async_copy(g_ref.at[j_me], recv.at[me_s], loc_sem)
    for i in range(half):
        mine, j, copy = outgoing(i)

        @pl.when(jnp.logical_not(mine))
        def _():
            copy.start()
        if i == 0:
            @pl.when(mine)
            def _():
                local.start()

    row_id = lax.broadcasted_iota(jnp.int32, (8, 128), 0)
    residue = j_me * 8 + row_id
    lane = lax.broadcasted_iota(jnp.int32, (8, 128), 1)
    for i in range(shots):
        s = lax.rem(me_s + i, shots)

        def arrive():
            pltpu.make_async_remote_copy(
                src_ref=g_ref.at[0], dst_ref=recv.at[s],
                send_sem=send_sem.at[0], recv_sem=recv_sem.at[s],
                device_id=(s, from_b), device_id_type=MESH).wait_recv()
        if i == 0:
            @pl.when(from_b != me_b)
            def _():
                arrive()

            @pl.when(from_b == me_b)
            def _():
                local.wait()
        else:
            arrive()
        upper = residue < offsets_ref[s, 0]
        right = lane < offsets_ref[s, 1]

        @pl.loop(0, 5 * rows // 8, unroll=4)
        def _(r):
            at = pl.ds(pl.multiple_of(r * 8, 8), 8)
            g = recv[s, at]
            hi = jnp.where(upper, g, 0.0)
            lo = jnp.where(upper, 0.0, g)
            for c, part in ((0, lo), (1, hi)):
                left_part = jnp.where(right, 0.0, part)
                right_part = jnp.where(right, part, 0.0)
                if i == 0:
                    acc[c, at, 0:128] = left_part
                    acc[c, at, 128:256] = right_part
                else:
                    acc[c, at, 0:128] += left_part
                    acc[c, at, 128:256] += right_part
    swaps = []
    for k in range(5):
        swaps.append(pltpu.make_async_remote_copy(
            src_ref=acc.at[1 - h, pl.ds(k * rows, rows)],
            dst_ref=out_ref.at[k, pl.ds(pl.multiple_of(h * rows, 8), rows)],
            send_sem=psend.at[k], recv_sem=precv.at[k],
            device_id=partner, device_id_type=MESH))
        swaps[k].start()
    for k in range(5):
        out_ref[k, pl.ds(pl.multiple_of(h * rows, 8), rows)] = acc[h, k * rows:(k + 1) * rows]
    for c in swaps:
        c.wait()
    for i in range(half):
        mine, j, copy = outgoing(i)

        @pl.when(jnp.logical_not(mine))
        def _():
            copy.wait_send()


def steps_kernel(param_ref, offsets_ref, sources_ref, traces_ref, state_ref, snap_ref, y1_ref,
                 final_ref, g_ref,
                 F, GZ, GY, ZZ, YY, ZY, SF, SG, COEF, ACC, TRIG, dbl, hsend, hrecv):
    me_s, me_b, half, h, j_me = where_am_i()
    slabs = 2 * half
    nz, nx, ny = state_ref.shape[1:]
    nt = snap_ref.shape[0]
    tiles = nx // 16
    ox = lax.rem(offsets_ref[me_s, 0], nx)
    oy = lax.rem(offsets_ref[me_s, 1], ny)
    has_up = me_b > 0
    has_down = me_b < slabs - 1
    up = (me_s, lax.max(me_b - 1, 0))
    down = (me_s, lax.min(me_b + 1, slabs - 1))

    barrier = pltpu.get_barrier_semaphore()

    @pl.when(has_up)
    def _():
        pl.semaphore_signal(barrier, inc=1, device_id=up, device_id_type=MESH)

    @pl.when(has_down)
    def _():
        pl.semaphore_signal(barrier, inc=1, device_id=down, device_id_type=MESH)
    pl.semaphore_wait(barrier, has_up.astype(jnp.int32) + has_down.astype(jnp.int32))

    for slot in range(2):
        for f in range(2):
            @pl.loop(0, nz + 8)
            def _(z):
                F[slot, f, z, 0:8] = jnp.zeros((8, ny), F32)
                F[slot, f, z, 8 + nx:16 + nx] = jnp.zeros((8, ny), F32)

            @pl.when(me_b == 0)
            def _():
                @pl.loop(0, 4)
                def _(z):
                    F[slot, f, z] = jnp.zeros((nx + 16, ny), F32)

            @pl.when(me_b == slabs - 1)
            def _():
                @pl.loop(nz + 4, nz + 8)
                def _(z):
                    F[slot, f, z] = jnp.zeros((nx + 16, ny), F32)

    for f in range(2):
        @pl.loop(0, nz)
        def _(z):
            now = state_ref[f, z]
            F[0, f, z + 4, 8:8 + nx] = now
            F[1, f, z + 4, 8:8 + nx] = state_ref[2 + f, z]
            hi = now.astype(BF16)
            at = pl.ds(pl.multiple_of((f * nz + z) * nx, 16), nx)
            SF[at, 0:ny] = hi
            SF[at, ny:2 * ny] = (now - hi.astype(F32)).astype(BF16)
            for g in (GZ, GY):
                g[f, z, 0:8] = jnp.zeros((8, ny), F32)
                g[f, z, 8 + nx:16 + nx] = jnp.zeros((8, ny), F32)

    def halo(slot, direction):
        rows = (pl.ds(4, 4), pl.ds(nz + 4, 4)) if direction == 0 else (pl.ds(nz, 4), pl.ds(0, 4))
        return pltpu.make_async_remote_copy(
            src_ref=F.at[slot, :, rows[0], pl.ds(8, nx)],
            dst_ref=F.at[slot, :, rows[1], pl.ds(8, nx)],
            send_sem=hsend.at[slot, direction], recv_sem=hrecv.at[slot, direction],
            device_id=(up, down)[direction], device_id_type=MESH)

    def send_halos(slot):
        @pl.when(has_up)
        def _():
            halo(slot, 0).start()

        @pl.when(has_down)
        def _():
            halo(slot, 1).start()

    def wait_halos(slot):
        @pl.when(has_up)
        def _():
            halo(slot, 0).wait_send()
            halo(slot, 1).wait_recv()

        @pl.when(has_down)
        def _():
            halo(slot, 1).wait_send()
            halo(slot, 0).wait_recv()

    send_halos(0)

    lane_shift = lax.rem(ny - oy, ny)
    for k in range(5):
        @pl.loop(0, nz // 2)
        def _(zz):
            for j in range(nx // 8):
                two = param_ref[j, pl.ds(pl.multiple_of(k * nz * 8 + zz * 16, 16), 16)].astype(F32)
                for half_row in range(2):
                    part = two[8 * half_row:8 * half_row + 8]
                    dbl[zz * 2 + half_row, 8 * j:8 * j + 8] = part
                    dbl[zz * 2 + half_row, nx + 8 * j:nx + 8 * j + 8] = part

        @pl.loop(0, nz)
        def _(z):
            TRIG[k, z] = pltpu.roll(dbl[z, pl.ds(ox, nx)], lane_shift, 1)

    source = sources_ref[0]
    first_row = me_b * nz

    @pl.loop(0, nz)
    def _(z):
        for t in range(tiles):
            at = pl.ds(16 * t, 16)
            v = TRIG[0, z, at]
            c = v * v
            a = 1.0 + 2.0 * TRIG[1, z, at]
            b = jnp.sqrt(1.0 + 2.0 * TRIG[2, z, at])
            st, ct = sine_cosine(TRIG[3, z, at])
            sa, ca = sine_cosine(TRIG[4, z, at])
            n_z, n_x, n_y = ct, st * ca, st * sa
            TRIG[1, z, at] = st
            TRIG[2, z, at] = ct
            TRIG[3, z, at] = sa
            TRIG[4, z, at] = ca
            mixed = 2.0 * UNIT11 / UNIT2
            COEF[0, z, at] = n_z * n_z
            COEF[1, z, at] = n_x * n_x
            COEF[2, z, at] = mixed * n_z * n_x
            COEF[3, z, at] = mixed * n_z * n_y
            COEF[4, z, at] = mixed * n_x * n_y
            COEF[5, z, at] = a
            COEF[6, z, at] = b
            COEF[7, z, at] = UNIT2 * c
            cell = (((first_row + z) * nx + 16 * t + lax.broadcasted_iota(jnp.int32, (16, ny), 0)) * ny
                    + lax.broadcasted_iota(jnp.int32, (16, ny), 1))
            COEF[8, z, at] = jnp.where(cell == source, c, 0.0)
            for n in range(8):
                ACC[n, z, at] = jnp.zeros((16, ny), F32)

    def step(t, carry):
        cur = lax.rem(t, 2)
        nxt = 1 - cur
        amplitude = traces_ref[0, t]
        for f in range(2):
            out = jnp.dot(SF[f * nz * nx:(f + 1) * nz * nx], y1_ref[...], preferred_element_type=F32)
            for z in range(nz):
                GY[f, z, 8:8 + nx] = out[z * nx:(z + 1) * nx, 0:ny]
                YY[f, z] = out[z * nx:(z + 1) * nx, ny:2 * ny]
        wait_halos(cur)
        for f in range(2):
            @pl.loop(0, tiles)
            def _(q):
                x0 = pl.multiple_of(8 + 16 * q, 8)
                row = [F[cur, f, z, pl.ds(x0, 16)] for z in range(nz + 8)]
                for z in range(nz):
                    ZZ[f, z, pl.ds(pl.multiple_of(16 * q, 16), 16)] = second(lambda k: row[z + 4 + k])
                    g = first(lambda k: row[z + 4 + k])
                    GZ[f, z, pl.ds(x0, 16)] = g
                    hi = g.astype(BF16)
                    at = pl.ds(pl.multiple_of((f * nz + z) * nx + 16 * q, 16), 16)
                    SG[at, 0:ny] = hi
                    SG[at, ny:2 * ny] = (g - hi.astype(F32)).astype(BF16)
        for f in range(2):
            out = jnp.dot(SG[f * nz * nx:(f + 1) * nz * nx], y1_ref[:, 0:ny], preferred_element_type=F32)
            for z in range(nz):
                ZY[f, z] = out[z * nx:(z + 1) * nx]

        @pl.loop(0, nz)
        def _(z):
            for q in range(tiles):
                at = pl.ds(16 * q, 16)

                def parts(f):
                    def x_of(ref, *lead):
                        return lambda k: ref[(*lead, pl.ds(8 + 16 * q + k, 16))]
                    yy = YY[f, z, at]
                    return (
                        ZZ[f, z, at] - yy,
                        second(x_of(F, cur, f, z + 4)) - yy,
                        first(x_of(GZ, f, z)),
                        ZY[f, z, at],
                        first(x_of(GY, f, z)),
                        yy,
                        F[cur, f, z + 4, pl.ds(8 + 16 * q, 16)],
                    )
                coef = [COEF[n, z, at] for n in range(5)]
                dp = parts(0)
                dq = parts(1)

                def weighted(d):
                    total = coef[0] * d[0]
                    for n in range(1, 5):
                        total = total + coef[n] * d[n]
                    return total
                base_p = dp[5] + CENTRE * dp[6]
                base_q = dq[5] + CENTRE * dq[6]
                h2 = (dp[0] + dp[1]) + (base_p + base_p) - weighted(dp)
                h1 = base_q + weighted(dq)
                a = COEF[5, z, at]
                b = COEF[6, z, at]
                c = COEF[7, z, at]
                pn = (dp[6] + dp[6]) - F[nxt, 0, z + 4, pl.ds(8 + 16 * q, 16)] + c * (a * h2 + b * h1)
                pn = pn + amplitude * COEF[8, z, at]
                qn = (dq[6] + dq[6]) - F[nxt, 1, z + 4, pl.ds(8 + 16 * q, 16)] + c * (b * h2 + h1)
                F[nxt, 0, z + 4, pl.ds(8 + 16 * q, 16)] = pn
                F[nxt, 1, z + 4, pl.ds(8 + 16 * q, 16)] = qn
                for f, value in ((0, pn), (1, qn)):
                    hi = value.astype(BF16)
                    rows = pl.ds(pl.multiple_of((f * nz + z) * nx + 16 * q, 16), 16)
                    SF[rows, 0:ny] = hi
                    SF[rows, ny:2 * ny] = (value - hi.astype(F32)).astype(BF16)
                pf = snap_ref[t, 0, z, at].astype(F32)
                qf = snap_ref[t, 1, z, at].astype(F32)
                bp = b * pf
                wa = a * pf + b * qf
                wb = bp + qf
                ACC[0, z, at] += h2 * wa + h1 * wb
                ACC[1, z, at] += h2 * pf
                ACC[2, z, at] += h1 * pf + h2 * qf
                for n in range(5):
                    ACC[3 + n, z, at] += dq[n] * wb - dp[n] * wa

        @pl.when(t < nt - 1)
        def _():
            send_halos(nxt)
        return carry

    lax.fori_loop(0, nt, step, 0)
    last = nt % 2
    for f in range(2):
        @pl.loop(0, nz)
        def _(z):
            final_ref[f, z] = F[last, f, z + 4, 8:8 + nx]

    back_shift = lax.rem(nx - ox, nx)

    def to_residues(k, value):
        for part in range(2):
            dbl[0, part * nx:(part + 1) * nx] = value
        return pltpu.roll(dbl[0, pl.ds(back_shift, nx)], oy, 1)

    @pl.loop(0, nz)
    def _(z):
        v = TRIG[0, z]
        st, ct, sa, ca = (TRIG[n, z] for n in range(1, 5))
        c = v * v
        b = COEF[6, z]
        n_z, n_x, n_y = ct, st * ca, st * sa
        x = [ACC[n, z] for n in range(8)]
        t_z, t_x, t_y = -st, ct * ca, ct * sa
        a_x, a_y = -st * sa, st * ca
        r = UNIT11 / UNIT2
        tilt = (t_z * n_z * x[3] + t_x * n_x * x[4]
                + r * ((t_z * n_x + t_x * n_z) * x[5] + (t_z * n_y + t_y * n_z) * x[6]
                       + (t_x * n_y + t_y * n_x) * x[7]))
        turn = (a_x * n_x * x[4]
                + r * (a_x * n_z * x[5] + a_y * n_z * x[6] + (a_x * n_y + a_y * n_x) * x[7]))
        sums = (
            2.0 * UNIT2 * v * x[0],
            2.0 * UNIT2 * c * x[1],
            UNIT2 * (c / b) * x[2],
            2.0 * UNIT2 * c * tilt,
            2.0 * UNIT2 * c * turn,
        )
        for k in range(5):
            out = to_residues(k, sums[k])
            for j in range(nx // 8):
                g_ref[j, pl.ds(pl.multiple_of(k * nz * 8 + z * 8, 8), 8)] = out[8 * j:8 * j + 8]


def y_matrix(ny):
    matrix = [[0.0] * (2 * ny) for _ in range(ny)]
    for y in range(ny):
        for k in range(1, 5):
            if y + k < ny:
                matrix[y + k][y] = FIRST[k - 1]
                matrix[y + k][ny + y] = SECOND[k - 1]
            if y - k >= 0:
                matrix[y - k][y] = -FIRST[k - 1]
                matrix[y - k][ny + y] = SECOND[k - 1]
    one = jnp.asarray(matrix, F32).astype(BF16)
    return jnp.concatenate([one, one], axis=0)


def on_device(velocity, epsilon, delta, tilt, azimuth, offsets, sources, traces, adjoint_state, snapshots):
    shots = lax.axis_size("shot")
    slabs = lax.axis_size("slab")
    half = slabs // 2
    _, _, nz, nx, ny = adjoint_state.shape
    nt = snapshots.shape[0]
    depth, width, lanes = velocity.shape
    rows = depth * width // 2
    vmem = pl.BlockSpec(memory_space=pltpu.VMEM)
    smem = pl.BlockSpec(memory_space=pltpu.SMEM)
    dma = pltpu.SemaphoreType.DMA
    params = [m.reshape(depth * width, lanes) for m in (velocity, epsilon, delta, tilt, azimuth)]
    residues = pl.pallas_call(
        fetch_kernel,
        out_shape=jax.ShapeDtypeStruct((half, 5 * rows, lanes // 2), BF16),
        in_specs=[vmem] * 5 + [smem],
        out_specs=vmem,
        scratch_shapes=[
            pltpu.VMEM((2, 5, rows, lanes), BF16),
            pltpu.VMEM((shots, 5 * rows, lanes // 2), BF16),
            dma((5,)), dma((5,)), dma((shots,)), dma((half,)), dma(()),
        ],
        compiler_params=pltpu.CompilerParams(collective_id=0, has_side_effects=True, vmem_limit_bytes=VMEM_LIMIT),
        name="fetch",
    )(*params, offsets)
    state = adjoint_state.reshape(4, nz, nx, ny)
    frames = snapshots.reshape(nt, 2, nz, nx, ny)
    final, sums = pl.pallas_call(
        steps_kernel,
        out_shape=(
            jax.ShapeDtypeStruct((2, nz, nx, ny), F32),
            jax.ShapeDtypeStruct((half, 5 * rows, ny), F32),
        ),
        in_specs=[vmem, smem, smem, smem, vmem, vmem, vmem],
        out_specs=(vmem, vmem),
        scratch_shapes=[
            pltpu.VMEM((2, 2, nz + 8, nx + 16, ny), F32),
            pltpu.VMEM((2, nz, nx + 16, ny), F32),
            pltpu.VMEM((2, nz, nx + 16, ny), F32),
            pltpu.VMEM((2, nz, nx, ny), F32),
            pltpu.VMEM((2, nz, nx, ny), F32),
            pltpu.VMEM((2, nz, nx, ny), F32),
            pltpu.VMEM((2 * nz * nx, 2 * ny), BF16),
            pltpu.VMEM((2 * nz * nx, 2 * ny), BF16),
            pltpu.VMEM((9, nz, nx, ny), F32),
            pltpu.VMEM((8, nz, nx, ny), F32),
            pltpu.VMEM((5, nz, nx, ny), F32),
            pltpu.VMEM((nz, 2 * nx, ny), F32),
            dma((2, 2)), dma((2, 2)),
        ],
        compiler_params=pltpu.CompilerParams(collective_id=1, has_side_effects=True, vmem_limit_bytes=VMEM_LIMIT),
        name="steps",
    )(residues, offsets, sources, traces, state, frames, y_matrix(ny))
    gradients = pl.pallas_call(
        return_kernel,
        out_shape=jax.ShapeDtypeStruct((5, 2 * rows, lanes), F32),
        in_specs=[vmem, smem],
        out_specs=vmem,
        scratch_shapes=[
            pltpu.VMEM((shots, 5 * rows, lanes // 2), F32),
            pltpu.VMEM((2, 5 * rows, lanes), F32),
            dma((half,)), dma((shots,)), dma(()), dma((5,)), dma((5,)),
        ],
        compiler_params=pltpu.CompilerParams(collective_id=2, has_side_effects=True, vmem_limit_bytes=VMEM_LIMIT),
        name="give_back",
    )(sums, offsets)
    return (gradients.reshape(5, depth, width, lanes), final.reshape(2, 1, nz, nx, ny))


def solution(mesh):
    return jax.shard_map(
        on_device,
        mesh=mesh,
        in_specs=(
            P("shot", "slab", None),
            P("shot", "slab", None),
            P("shot", "slab", None),
            P("shot", "slab", None),
            P("shot", "slab", None),
            P(),
            P("shot"),
            P("shot", None),
            P(None, "shot", "slab", None, None),
            P(None, None, "shot", "slab", None, None),
        ),
        out_specs=(P(None, "shot", "slab", None), P(None, "shot", "slab", None, None)),
        check_vma=False,
    )
```

```python
import functools
import jax
import jax.numpy as jnp
from jax import lax
from jax.sharding import PartitionSpec as P
from jax.experimental import pallas as pl
from jax.experimental.pallas import tpu as pltpu

MESH = pl.DeviceIdType.MESH
F32 = jnp.float32
BF16 = jnp.bfloat16

SECOND = (63.0, -7.875, 1.0, -9.0 / 128.0)
FIRST = (21.0, -5.25, 1.0, -3.0 / 32.0)
UNIT2 = 8.0 / 315.0
UNIT11 = (4.0 / 105.0) ** 2
CENTRE = -7175.0 / 64.0
UNROLL = 4
VMEM_LIMIT = 60 * 1024 * 1024


def second(at):
    total = at(3) + at(-3)
    for k in (1, 2, 4):
        total = total + SECOND[k - 1] * (at(k) + at(-k))
    return total


def first(at):
    total = at(3) - at(-3)
    for k in (1, 2, 4):
        total = total + FIRST[k - 1] * (at(k) - at(-k))
    return total


def sine_cosine(angle):
    u = 0.5 * angle
    w = u * u
    s = 1.0 / 362880.0 - w * (1.0 / 39916800.0)
    for term in (-1.0 / 5040.0, 1.0 / 120.0, -1.0 / 6.0, 1.0):
        s = term + w * s
    s = s * u
    c = -1.0 / 3628800.0 + w * (1.0 / 479001600.0)
    for term in (1.0 / 40320.0, -1.0 / 720.0, 1.0 / 24.0, -0.5, 1.0):
        c = term + w * c
    return 2.0 * s * c, 1.0 - 2.0 * s * s


def where_am_i():
    me_s = lax.axis_index("shot")
    me_b = lax.axis_index("slab")
    half = lax.axis_size("slab") // 2
    return me_s, me_b, half, me_b // half, lax.rem(me_b, half)


def fetch_kernel(v_ref, e_ref, d_ref, t_ref, a_ref, offsets_ref, out_ref,
                 both, sendbuf, psend, precv, send_sem, recv_sem, loc_sem):
    me_s, me_b, half, h, j_me = where_am_i()
    shots = lax.axis_size("shot")
    partner = (me_s, lax.rem(me_b + half, 2 * half))
    target = 2 * me_s + h
    is_self = target == me_b
    not_self = target != me_b
    rows = sendbuf.shape[1] // 5
    src_s, src_h = me_b // 2, lax.rem(me_b, 2)

    barrier = pltpu.get_barrier_semaphore()
    pl.semaphore_signal(barrier, inc=1, device_id=partner, device_id_type=MESH)
    for j in range(half):
        src_b = src_h * half + j

        @pl.when((src_s != me_s) | (src_b != me_b))
        def _():
            pl.semaphore_signal(barrier, inc=1, device_id=(src_s, src_b), device_id_type=MESH)
    pl.semaphore_wait(barrier, 1 + shots - is_self.astype(jnp.int32))

    params = (v_ref, e_ref, d_ref, t_ref, a_ref)
    theirs = pl.ds(pl.multiple_of(rows * (1 - h), 16), rows)
    ours = pl.ds(pl.multiple_of(rows * h, 16), rows)
    swaps = [
        pltpu.make_async_remote_copy(
            src_ref=params[k].at[theirs], dst_ref=both.at[h, k],
            send_sem=psend.at[k], recv_sem=precv.at[k],
            device_id=partner, device_id_type=MESH)
        for k in range(5)
    ]
    for c in swaps:
        c.start()
    for k in range(5):
        both[h, k] = params[k][ours]
    for c in swaps:
        c.wait()

    row_id = lax.broadcasted_iota(jnp.int32, (16, 128), 0)
    residue = j_me * 8 + lax.rem(row_id, 8)
    lane = lax.broadcasted_iota(jnp.int32, (16, 128), 1)

    def outgoing(i):
        s = lax.rem(me_s + i, shots)
        return s, pltpu.make_async_remote_copy(
            src_ref=sendbuf.at[i], dst_ref=out_ref.at[j_me],
            send_sem=send_sem.at[i], recv_sem=recv_sem.at[j_me],
            device_id=(s, target), device_id_type=MESH)

    local = pltpu.make_async_copy(sendbuf.at[0], out_ref.at[j_me], loc_sem)
    for i in range(shots):
        s, copy = outgoing(i)
        upper = residue < offsets_ref[s, 0]
        right = lane < offsets_ref[s, 1]
        for k in range(5):
            @pl.loop(0, rows // 16)
            def _(r):
                at = pl.ds(pl.multiple_of(r * 16, 16), 16)
                lo = both[0, k, at].astype(F32)
                hi = both[1, k, at].astype(F32)
                left_part = jnp.where(upper, hi[:, :128], lo[:, :128])
                right_part = jnp.where(upper, hi[:, 128:], lo[:, 128:])
                sendbuf[i, pl.ds(pl.multiple_of(k * rows + r * 16, 16), 16)] = (
                    jnp.where(right, right_part, left_part).astype(BF16))
        if i == 0:
            @pl.when(not_self)
            def _():
                copy.start()

            @pl.when(is_self)
            def _():
                local.start()
        else:
            copy.start()
    for i in range(shots):
        s, copy = outgoing(i)
        if i == 0:
            @pl.when(not_self)
            def _():
                copy.wait_send()

            @pl.when(is_self)
            def _():
                local.wait()
        else:
            copy.wait_send()
    for j in range(half):
        @pl.when((src_s != me_s) | (src_h * half + j != me_b))
        def _():
            pltpu.make_async_remote_copy(
                src_ref=sendbuf.at[0], dst_ref=out_ref.at[j],
                send_sem=send_sem.at[0], recv_sem=recv_sem.at[j],
                device_id=(src_s, src_h * half + j), device_id_type=MESH).wait_recv()


def return_kernel(g_ref, offsets_ref, out_ref, first_in, second_in, third_in, acc,
                  send_sem, recv_sem, loc_sem, psend, precv):
    me_s, me_b, half, h, j_me = where_am_i()
    shots = lax.axis_size("shot")
    partner = (me_s, lax.rem(me_b + half, 2 * half))
    rows = out_ref.shape[1] // 2
    x, y_hi, y_lo = me_s // 2, lax.rem(me_s, 2), h
    z, core = j_me // 2, lax.rem(j_me, 2)
    columns = shots // 2

    barrier = pltpu.get_barrier_semaphore()
    count = 0
    for i in range(1, half):
        pl.semaphore_signal(barrier, inc=1, device_id=(me_s, y_lo * half + lax.rem(j_me + i, half)),
                            device_id_type=MESH)
        count += 1
    for i in range(1, 4):
        y = lax.rem(y_hi * 2 + y_lo + i, 4)
        pl.semaphore_signal(barrier, inc=1, device_id=(x * 2 + y // 2, lax.rem(y, 2) * half + j_me),
                            device_id_type=MESH)
        count += 1
    for i in range(1, columns):
        pl.semaphore_signal(barrier, inc=1, device_id=(lax.rem(x + i, columns) * 2 + y_hi, me_b),
                            device_id_type=MESH)
        count += 1
    pl.semaphore_wait(barrier, count)

    def remote(stage, i, source, target_slot, device):
        return pltpu.make_async_remote_copy(
            src_ref=source, dst_ref=target_slot, send_sem=send_sem.at[stage, i],
            recv_sem=recv_sem.at[stage, i], device_id=device, device_id_type=MESH)

    def along_z(i):
        j = lax.rem(j_me + i, half)
        return pltpu.make_async_remote_copy(
            src_ref=g_ref.at[j], dst_ref=first_in.at[j_me], send_sem=send_sem.at[0, j],
            recv_sem=recv_sem.at[0, j_me], device_id=(me_s, y_lo * half + j), device_id_type=MESH)

    own = pltpu.make_async_copy(g_ref.at[j_me], first_in.at[j_me], loc_sem.at[0])
    own.start()
    for i in range(1, half):
        along_z(i).start()

    def along_y(i):
        j = lax.rem(j_me + i, half)
        z1, z0, c = j // 4, lax.rem(j // 2, 2), lax.rem(j, 2)
        slot = (y_hi * 2 + y_lo) * 2 + z1
        stays = (z0 == y_hi) & (c == y_lo)
        moves = (z0 != y_hi) | (c != y_lo)
        go = pltpu.make_async_remote_copy(
            src_ref=first_in.at[j], dst_ref=second_in.at[slot], send_sem=send_sem.at[1, j],
            recv_sem=recv_sem.at[1, slot], device_id=(x * 2 + z0, c * half + j_me), device_id_type=MESH)
        stay = pltpu.make_async_copy(first_in.at[j], second_in.at[slot], loc_sem.at[1 + z1])
        return stays, moves, go, stay

    for i in range(half):
        j = lax.rem(j_me + half - i, half)
        if i == 0:
            own.wait()
        else:
            pltpu.make_async_remote_copy(
                src_ref=g_ref.at[j], dst_ref=first_in.at[j], send_sem=send_sem.at[0, j],
                recv_sem=recv_sem.at[0, j], device_id=(me_s, y_lo * half + j), device_id_type=MESH).wait_recv()
        stays, moves, go, stay = along_y(half - i if i else 0)
        pl.when(moves)(go.start)
        pl.when(stays)(stay.start)

    def along_x(i):
        slot_in = lax.rem((y_hi * 2 + y_lo) * 2 + i, 8)
        from_hi, from_lo, z1 = slot_in // 4, lax.rem(slot_in // 2, 2), lax.rem(slot_in, 2)
        to_x = 2 * from_lo + z1
        shot = x * 2 + from_hi
        go = pltpu.make_async_remote_copy(
            src_ref=second_in.at[slot_in], dst_ref=third_in.at[shot], send_sem=send_sem.at[2, slot_in],
            recv_sem=recv_sem.at[2, shot], device_id=(to_x * 2 + y_hi, me_b), device_id_type=MESH)
        stay = pltpu.make_async_copy(second_in.at[slot_in], third_in.at[shot], loc_sem.at[3 + from_hi])
        return to_x == x, to_x != x, go, stay

    def from_y(i):
        slot_in = lax.rem((y_hi * 2 + y_lo) * 2 + i, 8)
        from_hi, from_lo, z1 = slot_in // 4, lax.rem(slot_in // 2, 2), lax.rem(slot_in, 2)
        return pltpu.make_async_remote_copy(
            src_ref=first_in.at[0], dst_ref=second_in.at[slot_in], send_sem=send_sem.at[1, 0],
            recv_sem=recv_sem.at[1, slot_in], device_id=(x * 2 + from_hi, from_lo * half + j_me),
            device_id_type=MESH)

    for i in range(8):
        if i < 2:
            slot_in = (y_hi * 2 + y_lo) * 2 + i
            pltpu.make_async_copy(first_in.at[0], second_in.at[slot_in], loc_sem.at[1 + i]).wait()
        else:
            from_y(i).wait_recv()
        stays, moves, go, stay = along_x(i)
        pl.when(moves)(go.start)
        pl.when(stays)(stay.start)

    for i in range(shots):
        s = lax.rem(me_s + i, shots)
        from_hi = lax.rem(s, 2)
        if i == 0 or i == 1:
            pass
        here = s // 2 == x
        away = s // 2 != x

        @pl.when(here)
        def _():
            pltpu.make_async_copy(second_in.at[0], third_in.at[s], loc_sem.at[3 + from_hi]).wait()

        @pl.when(away)
        def _():
            pltpu.make_async_remote_copy(
                src_ref=second_in.at[0], dst_ref=third_in.at[s], send_sem=send_sem.at[2, 0],
                recv_sem=recv_sem.at[2, s], device_id=(s // 2 * 2 + y_hi, me_b), device_id_type=MESH).wait_recv()

    row_id = lax.broadcasted_iota(jnp.int32, (16, 128), 0)
    residue = j_me * 8 + lax.rem(row_id, 8)
    lane = lax.broadcasted_iota(jnp.int32, (16, 128), 1)

    def swap(k):
        return pltpu.make_async_remote_copy(
            src_ref=acc.at[1 - h, k],
            dst_ref=out_ref.at[k, pl.ds(pl.multiple_of(h * rows, 8), rows)],
            send_sem=psend.at[k], recv_sem=precv.at[k],
            device_id=partner, device_id_type=MESH)

    for k in range(5):
        scales, uppers, rights = [], [], []
        for s in range(shots):
            exponents = third_in[s, 5 * rows:5 * rows + 16].astype(jnp.int32).astype(F32)
            scales.append(jnp.broadcast_to(jnp.exp2(exponents[k:k + 1] - 14.9), (16, 128)))
            uppers.append(residue < offsets_ref[s, 0])
            rights.append(lane < offsets_ref[s, 1])

        @pl.loop(0, rows // 16)
        def _(r):
            at = pl.ds(pl.multiple_of(r * 16, 16), 16)
            total = [[0.0, 0.0], [0.0, 0.0]]
            for s in range(shots):
                g = third_in[s, pl.ds(pl.multiple_of(k * rows + r * 16, 16), 16)].astype(jnp.int32).astype(F32)
                g = g * scales[s]
                hi = jnp.where(uppers[s], g, 0.0)
                for c, part in ((0, g - hi), (1, hi)):
                    right_part = jnp.where(rights[s], part, 0.0)
                    total[c][1] = total[c][1] + right_part
                    total[c][0] = total[c][0] + (part - right_part)
            for c in range(2):
                acc[c, k, at, 0:128] = total[c][0]
                acc[c, k, at, 128:256] = total[c][1]
        swap(k).start()
        out_ref[k, pl.ds(pl.multiple_of(h * rows, 8), rows)] = acc[h, k]
    for k in range(5):
        swap(k).wait()
    for i in range(1, half):
        along_z(i).wait_send()
    for i in range(half):
        stays, moves, go, stay = along_y(i)
        pl.when(moves)(go.wait_send)
    for i in range(8):
        stays, moves, go, stay = along_x(i)
        pl.when(moves)(go.wait_send)


def steps_kernel(param_ref, offsets_ref, sources_ref, traces_ref, state_ref, snap_ref, y1_ref,
                 final_ref, g_ref,
                 F, GZ, GY, ZZ, YY, ZY, SF, SG, COEF, ACC, TRIG, dbl, hsend, hrecv):
    me_s, me_b, half, h, j_me = where_am_i()
    slabs = 2 * half
    nz, nx, ny = state_ref.shape[1:]
    nt = snap_ref.shape[0]
    tiles = nx // 16
    ox = lax.rem(offsets_ref[me_s, 0], nx)
    oy = lax.rem(offsets_ref[me_s, 1], ny)
    has_up = me_b > 0
    has_down = me_b < slabs - 1
    up = (me_s, lax.max(me_b - 1, 0))
    down = (me_s, lax.min(me_b + 1, slabs - 1))

    barrier = pltpu.get_barrier_semaphore()

    @pl.when(has_up)
    def _():
        pl.semaphore_signal(barrier, inc=1, device_id=up, device_id_type=MESH)

    @pl.when(has_down)
    def _():
        pl.semaphore_signal(barrier, inc=1, device_id=down, device_id_type=MESH)
    pl.semaphore_wait(barrier, has_up.astype(jnp.int32) + has_down.astype(jnp.int32))

    for slot in range(2):
        for f in range(2):
            @pl.loop(0, nz + 8)
            def _(z):
                F[slot, f, z, 0:8] = jnp.zeros((8, ny), F32)
                F[slot, f, z, 8 + nx:16 + nx] = jnp.zeros((8, ny), F32)

            @pl.when(me_b == 0)
            def _():
                @pl.loop(0, 4)
                def _(z):
                    F[slot, f, z] = jnp.zeros((nx + 16, ny), F32)

            @pl.when(me_b == slabs - 1)
            def _():
                @pl.loop(nz + 4, nz + 8)
                def _(z):
                    F[slot, f, z] = jnp.zeros((nx + 16, ny), F32)

    for f in range(2):
        @pl.loop(0, nz)
        def _(z):
            now = state_ref[f, z]
            F[0, f, z + 4, 8:8 + nx] = now
            F[1, f, z + 4, 8:8 + nx] = state_ref[2 + f, z]
            hi = now.astype(BF16)
            at = pl.ds(pl.multiple_of((f * nz + z) * nx, 16), nx)
            SF[at, 0:ny] = hi
            SF[at, ny:2 * ny] = (now - hi.astype(F32)).astype(BF16)
            for g in (GZ, GY):
                g[f, z, 0:8] = jnp.zeros((8, ny), F32)
                g[f, z, 8 + nx:16 + nx] = jnp.zeros((8, ny), F32)

    def halo(slot, direction, q):
        rows = (pl.ds(4, 4), pl.ds(nz + 4, 4)) if direction == 0 else (pl.ds(nz, 4), pl.ds(0, 4))
        return pltpu.make_async_remote_copy(
            src_ref=F.at[slot, :, rows[0], pl.ds(8 + 16 * q, 16)],
            dst_ref=F.at[slot, :, rows[1], pl.ds(8 + 16 * q, 16)],
            send_sem=hsend.at[slot, direction, q], recv_sem=hrecv.at[slot, direction, q],
            device_id=(up, down)[direction], device_id_type=MESH)

    def send_halos(slot, q):
        @pl.when(has_up)
        def _():
            halo(slot, 0, q).start()

        @pl.when(has_down)
        def _():
            halo(slot, 1, q).start()

    def wait_halos(slot, q):
        @pl.when(has_up)
        def _():
            halo(slot, 0, q).wait_send()
            halo(slot, 1, q).wait_recv()

        @pl.when(has_down)
        def _():
            halo(slot, 1, q).wait_send()
            halo(slot, 0, q).wait_recv()

    for q in range(tiles):
        send_halos(0, q)

    lane_shift = lax.rem(ny - oy, ny)
    for k in range(5):
        @pl.loop(0, nz // 2)
        def _(zz):
            for j in range(nx // 8):
                two = param_ref[j, pl.ds(pl.multiple_of(k * nz * 8 + zz * 16, 16), 16)].astype(F32)
                for half_row in range(2):
                    part = two[8 * half_row:8 * half_row + 8]
                    dbl[zz * 2 + half_row, 8 * j:8 * j + 8] = part
                    dbl[zz * 2 + half_row, nx + 8 * j:nx + 8 * j + 8] = part

        @pl.loop(0, nz)
        def _(z):
            TRIG[k, z] = pltpu.roll(dbl[z, pl.ds(ox, nx)], lane_shift, 1)

    source = sources_ref[0]
    first_row = me_b * nz

    @pl.loop(0, nz)
    def _(z):
        for t in range(tiles):
            at = pl.ds(16 * t, 16)
            v = TRIG[0, z, at]
            c = v * v
            a = 1.0 + 2.0 * TRIG[1, z, at]
            b = jnp.sqrt(1.0 + 2.0 * TRIG[2, z, at])
            st, ct = sine_cosine(TRIG[3, z, at])
            sa, ca = sine_cosine(TRIG[4, z, at])
            n_z, n_x, n_y = ct, st * ca, st * sa
            TRIG[1, z, at] = st
            TRIG[2, z, at] = ct
            TRIG[3, z, at] = sa
            TRIG[4, z, at] = ca
            mixed = 2.0 * UNIT11 / UNIT2
            COEF[0, z, at] = n_z * n_z
            COEF[1, z, at] = n_x * n_x
            COEF[2, z, at] = mixed * n_z * n_x
            COEF[3, z, at] = mixed * n_z * n_y
            COEF[4, z, at] = mixed * n_x * n_y
            COEF[5, z, at] = a
            COEF[6, z, at] = b
            COEF[7, z, at] = UNIT2 * c
            cell = (((first_row + z) * nx + 16 * t + lax.broadcasted_iota(jnp.int32, (16, ny), 0)) * ny
                    + lax.broadcasted_iota(jnp.int32, (16, ny), 1))
            COEF[8, z, at] = jnp.where(cell == source, c, 0.0)
            for n in range(8):
                ACC[n, z, at] = jnp.zeros((16, ny), F32)

    def depth_pass(cur, q):
        wait_halos(cur, q)
        for f in range(2):
            row = [F[cur, f, z, 8 + 16 * q:24 + 16 * q] for z in range(nz + 8)]
            for z in range(nz):
                ZZ[f, z, 16 * q:16 * q + 16] = second(lambda k: row[z + 4 + k])
                g = first(lambda k: row[z + 4 + k])
                GZ[f, z, 8 + 16 * q:24 + 16 * q] = g
                hi = g.astype(BF16)
                at = (f * nz + z) * 16
                SG[q, at:at + 16, 0:ny] = hi
                SG[q, at:at + 16, ny:2 * ny] = (g - hi.astype(F32)).astype(BF16)

    def tile_pass(t, cur, nxt, q, amplitude):
        ZY[q] = jnp.dot(SG[q], y1_ref[:, 0:ny], preferred_element_type=F32)
        at = pl.ds(16 * q, 16)
        inner = pl.ds(8 + 16 * q, 16)

        @pl.loop(0, nz // UNROLL)
        def _(zz):
            for z_in in range(UNROLL):
                z = zz * UNROLL + z_in

                def parts(f):
                    def x_of(ref, *lead):
                        return lambda k: ref[(*lead, pl.ds(8 + 16 * q + k, 16))]
                    yy = YY[f, z, at]
                    return (
                        ZZ[f, z, at] - yy,
                        second(x_of(F, cur, f, z + 4)) - yy,
                        first(x_of(GZ, f, z)),
                        ZY[q, pl.ds(pl.multiple_of((f * nz + z) * 16, 16), 16)],
                        first(x_of(GY, f, z)),
                        yy,
                        F[cur, f, z + 4, inner],
                    )
                coef = [COEF[n, z, at] for n in range(5)]
                dp = parts(0)
                dq = parts(1)

                def weighted(d):
                    total = coef[0] * d[0]
                    for n in range(1, 5):
                        total = total + coef[n] * d[n]
                    return total
                base_p = dp[5] + CENTRE * dp[6]
                base_q = dq[5] + CENTRE * dq[6]
                h2 = (dp[0] + dp[1]) + (base_p + base_p) - weighted(dp)
                h1 = base_q + weighted(dq)
                a = COEF[5, z, at]
                b = COEF[6, z, at]
                c = COEF[7, z, at]
                pn = (dp[6] + dp[6]) - F[nxt, 0, z + 4, inner] + c * (a * h2 + b * h1)
                pn = pn + amplitude * COEF[8, z, at]
                qn = (dq[6] + dq[6]) - F[nxt, 1, z + 4, inner] + c * (b * h2 + h1)
                F[nxt, 0, z + 4, inner] = pn
                F[nxt, 1, z + 4, inner] = qn
                for f, value in ((0, pn), (1, qn)):
                    hi = value.astype(BF16)
                    rows = pl.ds(pl.multiple_of((f * nz + z) * nx + 16 * q, 16), 16)
                    SF[rows, 0:ny] = hi
                    SF[rows, ny:2 * ny] = (value - hi.astype(F32)).astype(BF16)
                pf = snap_ref[t, 0, z, at].astype(F32)
                qf = snap_ref[t, 1, z, at].astype(F32)
                bp = b * pf
                wa = a * pf + b * qf
                wb = bp + qf
                ACC[0, z, at] += h2 * wa + h1 * wb
                ACC[1, z, at] += h2 * pf
                ACC[2, z, at] += h1 * pf + h2 * qf
                for n in range(5):
                    ACC[3 + n, z, at] += dq[n] * wb - dp[n] * wa

        @pl.when(t < nt - 1)
        def _():
            send_halos(nxt, q)

    def step(t, carry):
        cur = lax.rem(t, 2)
        nxt = 1 - cur
        amplitude = traces_ref[0, t]
        for f in range(2):
            out = jnp.dot(SF[f * nz * nx:(f + 1) * nz * nx], y1_ref[...], preferred_element_type=F32)
            for z in range(nz):
                GY[f, z, 8:8 + nx] = out[z * nx:(z + 1) * nx, 0:ny]
                YY[f, z] = out[z * nx:(z + 1) * nx, ny:2 * ny]
        depth_pass(cur, 0)
        for q in range(tiles):
            if q + 1 < tiles:
                depth_pass(cur, q + 1)
            tile_pass(t, cur, nxt, q, amplitude)
        return carry

    lax.fori_loop(0, nt, step, 0)
    last = nt % 2
    for f in range(2):
        @pl.loop(0, nz)
        def _(z):
            final_ref[f, z] = F[last, f, z + 4, 8:8 + nx]

    back_shift = lax.rem(nx - ox, nx)

    def to_residues(k, value):
        for part in range(2):
            dbl[0, part * nx:(part + 1) * nx] = value
        return pltpu.roll(dbl[0, pl.ds(back_shift, nx)], oy, 1)

    @pl.loop(0, nz)
    def _(z):
        v = TRIG[0, z]
        st, ct, sa, ca = (TRIG[n, z] for n in range(1, 5))
        c = v * v
        b = COEF[6, z]
        n_z, n_x, n_y = ct, st * ca, st * sa
        x = [ACC[n, z] for n in range(8)]
        t_z, t_x, t_y = -st, ct * ca, ct * sa
        a_x, a_y = -st * sa, st * ca
        r = UNIT11 / UNIT2
        tilt = (t_z * n_z * x[3] + t_x * n_x * x[4]
                + r * ((t_z * n_x + t_x * n_z) * x[5] + (t_z * n_y + t_y * n_z) * x[6]
                       + (t_x * n_y + t_y * n_x) * x[7]))
        turn = (a_x * n_x * x[4]
                + r * (a_x * n_z * x[5] + a_y * n_z * x[6] + (a_x * n_y + a_y * n_x) * x[7]))
        sums = (
            2.0 * UNIT2 * v * x[0],
            2.0 * UNIT2 * c * x[1],
            UNIT2 * (c / b) * x[2],
            2.0 * UNIT2 * c * tilt,
            2.0 * UNIT2 * c * turn,
        )
        for k in range(5):
            TRIG[k, z] = to_residues(k, sums[k])

    encode(lambda k, z, j: TRIG[k, z, pl.ds(8 * j, 8)], g_ref, nx // 8, nz)


def encode(load, out_ref, blocks, nz):
    for j in range(blocks):
        exponents = []
        for k in range(5):
            largest = jnp.abs(load(k, 0, j))
            for z in range(1, nz):
                largest = jnp.maximum(largest, jnp.abs(load(k, z, j)))
            largest = jnp.max(largest, axis=0, keepdims=True)
            exponent = jnp.ceil(jnp.log2(jnp.maximum(largest, 1e-30))) + 0.0
            exponents.append(exponent)
            scale = jnp.broadcast_to(jnp.exp2(14.9 - exponent), (16, largest.shape[1]))
            for zz in range(nz // 2):
                pair = jnp.concatenate([load(k, 2 * zz, j), load(k, 2 * zz + 1, j)], axis=0)
                at = k * nz * 8 + zz * 16
                out_ref[j, at:at + 16] = jnp.round(pair * scale).astype(jnp.int32).astype(jnp.int16)
        rows = jnp.concatenate(exponents + [jnp.zeros_like(exponents[0])] * 11, axis=0)
        out_ref[j, 5 * nz * 8:5 * nz * 8 + 16] = rows.astype(jnp.int32).astype(jnp.int16)


def y_matrix(ny):
    matrix = [[0.0] * (2 * ny) for _ in range(ny)]
    for y in range(ny):
        for k in range(1, 5):
            if y + k < ny:
                matrix[y + k][y] = FIRST[k - 1]
                matrix[y + k][ny + y] = SECOND[k - 1]
            if y - k >= 0:
                matrix[y - k][y] = -FIRST[k - 1]
                matrix[y - k][ny + y] = SECOND[k - 1]
    one = jnp.asarray(matrix, F32).astype(BF16)
    return jnp.concatenate([one, one], axis=0)


def on_device(velocity, epsilon, delta, tilt, azimuth, offsets, sources, traces, adjoint_state, snapshots):
    shots = lax.axis_size("shot")
    slabs = lax.axis_size("slab")
    half = slabs // 2
    _, _, nz, nx, ny = adjoint_state.shape
    nt = snapshots.shape[0]
    depth, width, lanes = velocity.shape
    rows = depth * width // 2
    vmem = pl.BlockSpec(memory_space=pltpu.VMEM)
    smem = pl.BlockSpec(memory_space=pltpu.SMEM)
    dma = pltpu.SemaphoreType.DMA
    params = [m.reshape(depth * width, lanes) for m in (velocity, epsilon, delta, tilt, azimuth)]
    residues = pl.pallas_call(
        fetch_kernel,
        out_shape=jax.ShapeDtypeStruct((half, 5 * rows, lanes // 2), BF16),
        in_specs=[vmem] * 5 + [smem],
        out_specs=vmem,
        scratch_shapes=[
            pltpu.VMEM((2, 5, rows, lanes), BF16),
            pltpu.VMEM((shots, 5 * rows, lanes // 2), BF16),
            dma((5,)), dma((5,)), dma((shots,)), dma((half,)), dma(()),
        ],
        compiler_params=pltpu.CompilerParams(collective_id=0, has_side_effects=True, vmem_limit_bytes=VMEM_LIMIT),
        name="fetch",
    )(*params, offsets)
    state = adjoint_state.reshape(4, nz, nx, ny)
    frames = snapshots.reshape(nt, 2, nz, nx, ny)
    final, sums = pl.pallas_call(
        steps_kernel,
        out_shape=(
            jax.ShapeDtypeStruct((2, nz, nx, ny), F32),
            jax.ShapeDtypeStruct((half, 5 * rows + 16, ny), jnp.int16),
        ),
        in_specs=[vmem, smem, smem, smem, vmem, vmem, vmem],
        out_specs=(vmem, vmem),
        scratch_shapes=[
            pltpu.VMEM((2, 2, nz + 8, nx + 16, ny), F32),
            pltpu.VMEM((2, nz, nx + 16, ny), F32),
            pltpu.VMEM((2, nz, nx + 16, ny), F32),
            pltpu.VMEM((2, nz, nx, ny), F32),
            pltpu.VMEM((2, nz, nx, ny), F32),
            pltpu.VMEM((nx // 16, 2 * nz * 16, ny), F32),
            pltpu.VMEM((2 * nz * nx, 2 * ny), BF16),
            pltpu.VMEM((nx // 16, 2 * nz * 16, 2 * ny), BF16),
            pltpu.VMEM((9, nz, nx, ny), F32),
            pltpu.VMEM((8, nz, nx, ny), F32),
            pltpu.VMEM((5, nz, nx, ny), F32),
            pltpu.VMEM((nz, 2 * nx, ny), F32),
            dma((2, 2, nx // 16)), dma((2, 2, nx // 16)),
        ],
        compiler_params=pltpu.CompilerParams(collective_id=1, has_side_effects=True, vmem_limit_bytes=VMEM_LIMIT),
        name="steps",
    )(residues, offsets, sources, traces, state, frames, y_matrix(ny))
    gradients = pl.pallas_call(
        return_kernel,
        out_shape=jax.ShapeDtypeStruct((5, 2 * rows, lanes), F32),
        in_specs=[vmem, smem],
        out_specs=vmem,
        scratch_shapes=[
            pltpu.VMEM((half, 5 * rows + 16, ny), jnp.int16),
            pltpu.VMEM((8, 5 * rows + 16, ny), jnp.int16),
            pltpu.VMEM((shots, 5 * rows + 16, ny), jnp.int16),
            pltpu.VMEM((2, 5, rows, lanes), F32),
            dma((3, 8)), dma((3, 8)), dma((5,)), dma((5,)), dma((5,)),
        ],
        compiler_params=pltpu.CompilerParams(collective_id=2, has_side_effects=True, vmem_limit_bytes=VMEM_LIMIT),
        name="give_back",
    )(sums, offsets)
    return (gradients.reshape(5, depth, width, lanes), final.reshape(2, 1, nz, nx, ny))


def solution(mesh):
    return jax.shard_map(
        on_device,
        mesh=mesh,
        in_specs=(
            P("shot", "slab", None),
            P("shot", "slab", None),
            P("shot", "slab", None),
            P("shot", "slab", None),
            P("shot", "slab", None),
            P(),
            P("shot"),
            P("shot", None),
            P(None, "shot", "slab", None, None),
            P(None, None, "shot", "slab", None, None),
        ),
        out_specs=(P(None, "shot", "slab", None), P(None, "shot", "slab", None, None)),
        check_vma=False,
    )
```

```python
import functools
import jax
import jax.numpy as jnp
from jax import lax
from jax.sharding import PartitionSpec as P
from jax.experimental import pallas as pl
from jax.experimental.pallas import tpu as pltpu

MESH = pl.DeviceIdType.MESH
F32 = jnp.float32
BF16 = jnp.bfloat16

SECOND = (63.0, -7.875, 1.0, -9.0 / 128.0)
FIRST = (21.0, -5.25, 1.0, -3.0 / 32.0)
UNIT2 = 8.0 / 315.0
UNIT11 = (4.0 / 105.0) ** 2
CENTRE = -7175.0 / 64.0
EXPONENT_ROWS = 16
VMEM_LIMIT = 60 * 1024 * 1024


def second(at):
    total = at(3) + at(-3)
    for k in (1, 2, 4):
        total = total + SECOND[k - 1] * (at(k) + at(-k))
    return total


def first(at):
    total = at(3) - at(-3)
    for k in (1, 2, 4):
        total = total + FIRST[k - 1] * (at(k) - at(-k))
    return total


def sine_cosine(angle):
    u = 0.5 * angle
    w = u * u
    s = 1.0 / 362880.0 - w * (1.0 / 39916800.0)
    for term in (-1.0 / 5040.0, 1.0 / 120.0, -1.0 / 6.0, 1.0):
        s = term + w * s
    s = s * u
    c = -1.0 / 3628800.0 + w * (1.0 / 479001600.0)
    for term in (1.0 / 40320.0, -1.0 / 720.0, 1.0 / 24.0, -0.5, 1.0):
        c = term + w * c
    return 2.0 * s * c, 1.0 - 2.0 * s * s


def where_am_i():
    me_s = lax.axis_index("shot")
    me_b = lax.axis_index("slab")
    half = lax.axis_size("slab") // 2
    return me_s, me_b, half, me_b // half, lax.rem(me_b, half)


def remote(source, target, send, recv, device):
    return pltpu.make_async_remote_copy(
        src_ref=source, dst_ref=target, send_sem=send, recv_sem=recv, device_id=device, device_id_type=MESH)


def whole_kernel(v_ref, e_ref, d_ref, t_ref, a_ref, offsets_ref, sources_ref, traces_ref, state_ref, snap_hbm, y1_ref,
                 final_ref, out_ref,
                 both, sendbuf, pin, F, GZ, GY, ZZ, YY, ZY, SF, SG, COEF, ACC, TRIG, dbl, SNAP, MX,
                 GQ, first_in, second_in, third_in, acc, swap_out, swap_in,
                 in_sem, psend, precv, asend, arecv, aloc, hsend, hrecv, rsend, rrecv, rloc, ssend, srecv):
    me_s, me_b, half, h, j_me = where_am_i()
    shots = lax.axis_size("shot")
    slabs = 2 * half
    nz, nx, ny = state_ref.shape[1:]
    nt = SNAP.shape[0]
    tiles = nx // 16
    rows = nz * 8
    block = 2 * nz * 16
    partner = (me_s, lax.rem(me_b + half, slabs))
    x, y_hi, y_lo = me_s // 2, lax.rem(me_s, 2), h
    y_me = y_hi * 2 + y_lo
    columns = shots // 2

    target = 2 * me_s + h
    src_s, src_h = me_b // 2, lax.rem(me_b, 2)
    is_self = target == me_b
    not_self = target != me_b
    has_up = me_b > 0
    has_down = me_b < slabs - 1
    up = (me_s, lax.max(me_b - 1, 0))
    down = (me_s, lax.min(me_b + 1, slabs - 1))

    def z_line(i):
        return (me_s, y_lo * half + lax.rem(j_me + i, half))

    def y_line(i):
        y = lax.rem(y_me + i, 4)
        return (x * 2 + y // 2, lax.rem(y, 2) * half + j_me)

    def x_line(i):
        return (lax.rem(x + i, columns) * 2 + y_hi, me_b)

    barrier = pltpu.get_barrier_semaphore()

    def greet(device):
        pl.semaphore_signal(barrier, inc=1, device_id=device, device_id_type=MESH)

    for i in range(1, half):
        greet(z_line(i))
    for i in range(1, 4):
        greet(y_line(i))
    for i in range(1, columns):
        greet(x_line(i))
    pl.when(has_up)(lambda: greet(up))
    pl.when(has_down)(lambda: greet(down))
    for j in range(half):
        pl.when((src_s != me_s) | (src_h * half + j != me_b))(lambda: greet((src_s, src_h * half + j)))

    loads = [pltpu.make_async_copy(state_ref.at[n], F.at[n // 2, n % 2, pl.ds(4, nz), pl.ds(8, nx)], in_sem.at[n])
             for n in range(4)]
    loads.append(pltpu.make_async_copy(snap_hbm, SNAP, in_sem.at[4]))
    for c in loads:
        c.start()

    @pl.loop(0, nz + 8)
    def _(z):
        for slot in range(2):
            for f in range(2):
                F[slot, f, z, 0:8] = jnp.zeros((8, ny), F32)
                F[slot, f, z, 8 + nx:16 + nx] = jnp.zeros((8, ny), F32)

    @pl.loop(0, nz)
    def _(z):
        for f in range(2):
            for g in (GZ, GY.at[0], GY.at[1]):
                g[f, z, 0:8] = jnp.zeros((8, ny), F32)
                g[f, z, 8 + nx:16 + nx] = jnp.zeros((8, ny), F32)

    def clear(first_row):
        @pl.loop(0, 4)
        def _(z):
            for slot in range(2):
                for f in range(2):
                    F[slot, f, first_row + z] = jnp.zeros((nx + 16, ny), F32)

    pl.when(me_b == 0)(lambda: clear(0))
    pl.when(me_b == slabs - 1)(lambda: clear(nz + 4))

    pl.semaphore_wait(barrier, (half - 1) + 3 + (columns - 1) + has_up.astype(jnp.int32) + has_down.astype(jnp.int32)
                      + shots - is_self.astype(jnp.int32))

    params = (v_ref, e_ref, d_ref, t_ref, a_ref)
    theirs = pl.ds(pl.multiple_of(rows * (1 - h), 16), rows)
    ours = pl.ds(pl.multiple_of(rows * h, 16), rows)
    swaps = [remote(params[k].at[theirs], both.at[h, k], psend.at[k], precv.at[k], partner) for k in range(5)]
    for c in swaps:
        c.start()
    for k in range(5):
        both[h, k] = params[k][ours]

    def halo(slot, direction, q):
        rows = (pl.ds(4, 4), pl.ds(nz + 4, 4)) if direction == 0 else (pl.ds(nz, 4), pl.ds(0, 4))
        return remote(F.at[slot, :, rows[0], pl.ds(8 + 16 * q, 16)], F.at[slot, :, rows[1], pl.ds(8 + 16 * q, 16)],
                      hsend.at[slot, direction, q], hrecv.at[slot, direction, q], (up, down)[direction])

    def send_halos(slot, q):
        pl.when(has_up)(lambda: halo(slot, 0, q).start())
        pl.when(has_down)(lambda: halo(slot, 1, q).start())

    def wait_halos(slot, q):
        @pl.when(has_up)
        def _():
            halo(slot, 0, q).wait_send()
            halo(slot, 1, q).wait_recv()

        @pl.when(has_down)
        def _():
            halo(slot, 1, q).wait_send()
            halo(slot, 0, q).wait_recv()

    row_id = lax.broadcasted_iota(jnp.int32, (16, 128), 0)
    residue = j_me * 8 + lax.rem(row_id, 8)
    lane = lax.broadcasted_iota(jnp.int32, (16, 128), 1)

    def outgoing(i, k):
        s = lax.rem(me_s + i, shots)
        return remote(sendbuf.at[i, k], pin.at[j_me, k], asend.at[i, k], arecv.at[j_me, k], (s, target))

    def local(k):
        return pltpu.make_async_copy(sendbuf.at[0, k], pin.at[j_me, k], aloc.at[k])

    for k in range(5):
        swaps[k].wait()

        @pl.loop(0, rows // 16)
        def _(r):
            at = pl.ds(pl.multiple_of(r * 16, 16), 16)
            lo = both[0, k, at].astype(F32)
            hi = both[1, k, at].astype(F32)
            for i in range(shots):
                s = lax.rem(me_s + i, shots)
                upper = residue < offsets_ref[0, s]
                right = lane < offsets_ref[1, s]
                left_part = jnp.where(upper, hi[:, :128], lo[:, :128])
                right_part = jnp.where(upper, hi[:, 128:], lo[:, 128:])
                sendbuf[i, k, at] = jnp.where(right, right_part, left_part).astype(BF16)
        pl.when(not_self)(lambda: outgoing(0, k).start())
        pl.when(is_self)(lambda: local(k).start())
        for i in range(1, shots):
            outgoing(i, k).start()

    for c in loads[:4]:
        c.wait()
    for q in range(tiles):
        send_halos(0, q)

    def split(value, store):
        hi = value.astype(BF16)
        store(slice(0, ny), hi)
        store(slice(ny, 2 * ny), (value - hi.astype(F32)).astype(BF16))

    def along_y(slot, q):
        out = jnp.dot(SF[q], y1_ref[...], preferred_element_type=F32)
        for f in range(2):
            for z in range(nz):
                at = (f * nz + z) * 16
                GY[slot, f, z, 8 + 16 * q:24 + 16 * q] = out[at:at + 16, 0:ny]
                YY[slot, f, z, 16 * q:16 * q + 16] = out[at:at + 16, ny:2 * ny]

    for q in range(tiles):
        for f in range(2):
            @pl.loop(0, nz)
            def _(z):
                at = pl.ds(pl.multiple_of((f * nz + z) * 16, 16), 16)

                def store(lanes, value):
                    SF[q, at, lanes] = value
                split(F[0, f, z + 4, 8 + 16 * q:24 + 16 * q], store)
    for q in range(tiles - 1):
        along_y(0, q)

    ox = lax.rem(offsets_ref[0, me_s], nx)
    oy = lax.rem(offsets_ref[1, me_s], ny)
    lane_shift = lax.rem(ny - oy, ny)
    for k in range(5):
        for j in range(half):
            here = is_self & (j_me == j)
            away = not_self | (j_me != j)
            pl.when(here)(lambda: local(k).wait())
            pl.when(away)(lambda: remote(sendbuf.at[0, k], pin.at[j, k], asend.at[0, k], arecv.at[j, k],
                                         (src_s, src_h * half + j)).wait_recv())

        @pl.loop(0, nz // 2)
        def _(zz):
            for j in range(half):
                two = pin[j, k, pl.ds(pl.multiple_of(zz * 16, 16), 16)].astype(F32)
                for half_row in range(2):
                    part = two[8 * half_row:8 * half_row + 8]
                    dbl[zz * 2 + half_row, 8 * j:8 * j + 8] = part
                    dbl[zz * 2 + half_row, nx + 8 * j:nx + 8 * j + 8] = part

        @pl.loop(0, nz)
        def _(z):
            TRIG[k, z] = pltpu.roll(dbl[z, pl.ds(ox, nx)], lane_shift, 1)

    source = sources_ref[0]
    first_row = me_b * nz

    @pl.loop(0, nz)
    def _(z):
        for t in range(tiles):
            at = pl.ds(16 * t, 16)
            v = TRIG[0, z, at]
            c = v * v
            a = 1.0 + 2.0 * TRIG[1, z, at]
            b = jnp.sqrt(1.0 + 2.0 * TRIG[2, z, at])
            st, ct = sine_cosine(TRIG[3, z, at])
            sa, ca = sine_cosine(TRIG[4, z, at])
            n_z, n_x, n_y = ct, st * ca, st * sa
            TRIG[1, z, at] = st
            TRIG[2, z, at] = ct
            TRIG[3, z, at] = sa
            TRIG[4, z, at] = ca
            mixed = 2.0 * UNIT11 / UNIT2
            COEF[0, z, at] = n_z * n_z
            COEF[1, z, at] = n_x * n_x
            COEF[2, z, at] = mixed * n_z * n_x
            COEF[3, z, at] = mixed * n_z * n_y
            COEF[4, z, at] = mixed * n_x * n_y
            COEF[5, z, at] = a
            COEF[6, z, at] = b
            COEF[7, z, at] = UNIT2 * c
            cell = (((first_row + z) * nx + 16 * t + lax.broadcasted_iota(jnp.int32, (16, ny), 0)) * ny
                    + lax.broadcasted_iota(jnp.int32, (16, ny), 1))
            COEF[8, z, at] = jnp.where(cell == source, c, 0.0)
            for n in range(8):
                ACC[n, z, at] = jnp.zeros((16, ny), F32)

    loads[4].wait()

    def depth_pass(cur, q):
        for f in range(2):
            row = [F[cur, f, z, 8 + 16 * q:24 + 16 * q] for z in range(nz + 8)]
            for z in range(nz):
                ZZ[f, z, 16 * q:16 * q + 16] = second(lambda k: row[z + 4 + k])
                g = first(lambda k: row[z + 4 + k])
                GZ[f, z, 8 + 16 * q:24 + 16 * q] = g
                at = (f * nz + z) * 16

                def store(lanes, value):
                    SG[q, at:at + 16, lanes] = value
                split(g, store)

    def update(t, cur, nxt, q, z, amplitude):
        at = pl.ds(16 * q, 16)
        inner = pl.ds(8 + 16 * q, 16)

        def parts(f):
            def x_of(ref, *lead):
                return lambda k: ref[(*lead, pl.ds(8 + 16 * q + k, 16))]
            yy = YY[cur, f, z, at]
            return (
                ZZ[f, z, at] - yy,
                second(x_of(F, cur, f, z + 4)) - yy,
                first(x_of(GZ, f, z)),
                ZY[q, pl.ds(pl.multiple_of((f * nz + z) * 16, 16), 16)],
                first(x_of(GY, cur, f, z)),
                yy,
                F[cur, f, z + 4, inner],
            )
        coef = [COEF[n, z, at] for n in range(5)]
        dp = parts(0)
        dq = parts(1)

        def weighted(d):
            total = coef[0] * d[0]
            for n in range(1, 5):
                total = total + coef[n] * d[n]
            return total
        base_p = dp[5] + CENTRE * dp[6]
        base_q = dq[5] + CENTRE * dq[6]
        h2 = (dp[0] + dp[1]) + (base_p + base_p) - weighted(dp)
        h1 = base_q + weighted(dq)
        a = COEF[5, z, at]
        b = COEF[6, z, at]
        c = COEF[7, z, at]
        pn = (dp[6] + dp[6]) - F[nxt, 0, z + 4, inner] + c * (a * h2 + b * h1)
        pn = pn + amplitude * COEF[8, z, at]
        qn = (dq[6] + dq[6]) - F[nxt, 1, z + 4, inner] + c * (b * h2 + h1)
        F[nxt, 0, z + 4, inner] = pn
        F[nxt, 1, z + 4, inner] = qn
        for f, value in ((0, pn), (1, qn)):
            def store(lanes, part):
                SF[q, pl.ds(pl.multiple_of((f * nz + z) * 16, 16), 16), lanes] = part
            split(value, store)
        pf = SNAP[t, 0, z, at].astype(F32)
        qf = SNAP[t, 1, z, at].astype(F32)
        bp = b * pf
        wa = a * pf + b * qf
        wb = bp + qf
        ACC[0, z, at] += h2 * wa + h1 * wb
        ACC[1, z, at] += h2 * pf
        ACC[2, z, at] += h1 * pf + h2 * qf
        for n in range(5):
            ACC[3 + n, z, at] += dq[n] * wb - dp[n] * wa

    def step(t, carry):
        cur = lax.rem(t, 2)
        nxt = 1 - cur
        amplitude = traces_ref[0, t]
        wait_halos(cur, 0)
        along_y(cur, tiles - 1)
        depth_pass(cur, 0)
        for q in range(tiles):
            if q + 1 < tiles:
                wait_halos(cur, q + 1)
                depth_pass(cur, q + 1)
            ZY[q] = jnp.dot(SG[q], y1_ref[:, 0:ny], preferred_element_type=F32)
            if q > 0:
                along_y(nxt, q - 1)

            @pl.loop(0, 2)
            def _(zz):
                for z in range(4):
                    update(t, cur, nxt, q, zz * 8 + z, amplitude)
            pl.when(t < nt - 1)(lambda: send_halos(nxt, q))
            for z in range(4, 8):
                update(t, cur, nxt, q, z, amplitude)
        return carry

    lax.fori_loop(0, nt, step, 0)
    last = nt % 2
    for f in range(2):
        @pl.loop(0, nz)
        def _(z):
            final_ref[f, z] = F[last, f, z + 4, 8:8 + nx]

    back_shift = lax.rem(nx - ox, nx)
    MX[...] = jnp.zeros_like(MX)

    @pl.loop(0, nz)
    def _(z):
        v = TRIG[0, z]
        st, ct, sa, ca = (TRIG[n, z] for n in range(1, 5))
        c = v * v
        b = COEF[6, z]
        n_z, n_x, n_y = ct, st * ca, st * sa
        g = [ACC[n, z] for n in range(8)]
        t_z, t_x, t_y = -st, ct * ca, ct * sa
        a_x, a_y = -st * sa, st * ca
        r = UNIT11 / UNIT2
        tilt = (t_z * n_z * g[3] + t_x * n_x * g[4]
                + r * ((t_z * n_x + t_x * n_z) * g[5] + (t_z * n_y + t_y * n_z) * g[6]
                       + (t_x * n_y + t_y * n_x) * g[7]))
        turn = (a_x * n_x * g[4]
                + r * (a_x * n_z * g[5] + a_y * n_z * g[6] + (a_x * n_y + a_y * n_x) * g[7]))
        sums = (
            2.0 * UNIT2 * v * g[0],
            2.0 * UNIT2 * c * g[1],
            UNIT2 * (c / b) * g[2],
            2.0 * UNIT2 * c * tilt,
            2.0 * UNIT2 * c * turn,
        )
        for k in range(5):
            for part in range(2):
                dbl[k, part * nx:(part + 1) * nx] = sums[k]
        for k in range(5):
            value = pltpu.roll(dbl[k, pl.ds(back_shift, nx)], oy, 1)
            TRIG[k, z] = value
            MX[k] = jnp.maximum(MX[k], jnp.abs(value))

    def exponent_of(largest):
        return jnp.ceil(jnp.log2(jnp.maximum(jnp.max(largest, axis=0, keepdims=True), 1e-30)))

    def exponent_rows(exponents):
        rest = [jnp.zeros_like(exponents[0])] * (EXPONENT_ROWS - len(exponents))
        return jnp.concatenate(exponents + rest, axis=0).astype(jnp.int32).astype(jnp.int16)

    def coded(value):
        return jnp.round(value).astype(jnp.int32).astype(jnp.int16)

    for j in range(half):
        exponents = []
        for k in range(5):
            exponents.append(exponent_of(MX[k, 8 * j:8 * j + 8]))
            MX[k, 8 * j:8 * j + 8] = jnp.broadcast_to(jnp.exp2(14.9 - exponents[k]), (8, ny))
        GQ[j, 0:EXPONENT_ROWS] = exponent_rows(exponents)

    def chunk(k):
        return pl.ds(0, EXPONENT_ROWS + rows) if k == 0 else pl.ds(EXPONENT_ROWS + k * rows, rows)

    def hop_z(k, i):
        j = lax.rem(j_me + i, half)
        return remote(GQ.at[j, chunk(k)], first_in.at[j_me, chunk(k)], rsend.at[0, k, j], rrecv.at[0, k, j_me],
                      (me_s, y_lo * half + j))

    def own_z(k):
        return pltpu.make_async_copy(GQ.at[j_me, chunk(k)], first_in.at[j_me, chunk(k)], rloc.at[k, 0])

    for k in range(5):
        @pl.loop(0, nz // 2)
        def _(zz):
            for j in range(half):
                scale = MX[k, 8 * j:8 * j + 8]
                pair = jnp.concatenate([TRIG[k, 2 * zz, 8 * j:8 * j + 8] * scale,
                                        TRIG[k, 2 * zz + 1, 8 * j:8 * j + 8] * scale], axis=0)
                GQ[j, pl.ds(pl.multiple_of(EXPONENT_ROWS + k * rows + zz * 16, 16), 16)] = coded(pair)
        own_z(k).start()
        for i in range(1, half):
            hop_z(k, i).start()

    def hop_y(k, i):
        j = lax.rem(j_me + i, half)
        z1, z0, c = j // 4, lax.rem(j // 2, 2), lax.rem(j, 2)
        slot = y_me * 2 + z1
        go = remote(first_in.at[j, chunk(k)], second_in.at[slot, chunk(k)], rsend.at[1, k, j], rrecv.at[1, k, slot],
                    (x * 2 + z0, c * half + j_me))
        stay = pltpu.make_async_copy(first_in.at[j, chunk(k)], second_in.at[slot, chunk(k)], rloc.at[k, 1 + z1])
        return (z0 == y_hi) & (c == y_lo), (z0 != y_hi) | (c != y_lo), go, stay

    def forward_y(k):
        for i in range(half):
            j = lax.rem(j_me + i, half)
            if i == 0:
                own_z(k).wait()
            else:
                remote(GQ.at[j, chunk(k)], first_in.at[j, chunk(k)], rsend.at[0, k, j], rrecv.at[0, k, j],
                       (me_s, y_lo * half + j)).wait_recv()
            stays, moves, go, stay = hop_y(k, i)
            pl.when(moves)(go.start)
            pl.when(stays)(stay.start)

    def hop_x(k, i):
        slot = lax.rem(y_me * 2 + i, 8)
        from_hi, from_lo, z1 = slot // 4, lax.rem(slot // 2, 2), lax.rem(slot, 2)
        to_x = 2 * from_lo + z1
        shot = x * 2 + from_hi
        go = remote(second_in.at[slot, chunk(k)], third_in.at[shot, chunk(k)], rsend.at[2, k, slot],
                    rrecv.at[2, k, shot], (to_x * 2 + y_hi, me_b))
        stay = pltpu.make_async_copy(second_in.at[slot, chunk(k)], third_in.at[shot, chunk(k)],
                                     rloc.at[k, 3 + from_hi])
        return to_x == x, to_x != x, go, stay

    def forward_x(k):
        for i in range(8):
            slot = lax.rem(y_me * 2 + i, 8)
            if i < 2:
                pltpu.make_async_copy(first_in.at[0, chunk(k)], second_in.at[slot, chunk(k)], rloc.at[k, 1 + i]).wait()
            else:
                from_hi, from_lo = slot // 4, lax.rem(slot // 2, 2)
                remote(first_in.at[0, chunk(k)], second_in.at[slot, chunk(k)], rsend.at[1, k, 0],
                       rrecv.at[1, k, slot], (x * 2 + from_hi, from_lo * half + j_me)).wait_recv()
            stays, moves, go, stay = hop_x(k, i)
            pl.when(moves)(go.start)
            pl.when(stays)(stay.start)

    def swap(k):
        return remote(swap_out.at[k], swap_in.at[k], ssend.at[k], srecv.at[k], partner)

    def gather(k):
        for i in range(shots):
            s = lax.rem(me_s + i, shots)
            here = s // 2 == x
            away = s // 2 != x
            pl.when(here)(lambda: pltpu.make_async_copy(
                second_in.at[0, chunk(k)], third_in.at[s, chunk(k)], rloc.at[k, 3 + lax.rem(s, 2)]).wait())
            pl.when(away)(lambda: remote(
                second_in.at[0, chunk(k)], third_in.at[s, chunk(k)], rsend.at[2, k, 0], rrecv.at[2, k, s],
                (s // 2 * 2 + y_hi, me_b)).wait_recv())
        scales = []
        for s in range(shots):
            exponents = third_in[s, 0:EXPONENT_ROWS].astype(jnp.int32).astype(F32)
            scales.append(jnp.broadcast_to(jnp.exp2(exponents[k:k + 1] - 14.9), (16, 128)))

        @pl.loop(0, rows // 16)
        def _(r):
            at = pl.ds(pl.multiple_of(r * 16, 16), 16)
            total = [[0.0, 0.0], [0.0, 0.0]]
            for s in range(shots):
                upper = residue < offsets_ref[0, s]
                right = lane < offsets_ref[1, s]
                g = third_in[s, pl.ds(pl.multiple_of(EXPONENT_ROWS + k * rows + r * 16, 16), 16)]
                g = g.astype(jnp.int32).astype(F32) * scales[s]
                hi = jnp.where(upper, g, 0.0)
                for c, part in ((0, g - hi), (1, hi)):
                    right_part = jnp.where(right, part, 0.0)
                    total[c][1] = total[c][1] + right_part
                    total[c][0] = total[c][0] + (part - right_part)
            for c in range(2):
                acc[c, k, at, 0:128] = total[c][0]
                acc[c, k, at, 128:256] = total[c][1]
        largest = jnp.abs(acc[1 - h, k, 0:8])
        for r in range(1, rows // 8):
            largest = jnp.maximum(largest, jnp.abs(acc[1 - h, k, 8 * r:8 * r + 8]))
        exponent = exponent_of(largest)
        swap_out[k, 0:EXPONENT_ROWS] = exponent_rows([exponent])
        scale = jnp.broadcast_to(jnp.exp2(14.9 - exponent), (16, 2 * ny))

        @pl.loop(0, rows // 16)
        def _(r):
            at = pl.ds(pl.multiple_of(r * 16, 16), 16)
            swap_out[k, pl.ds(pl.multiple_of(EXPONENT_ROWS + r * 16, 16), 16)] = coded(acc[1 - h, k, at] * scale)
        swap(k).start()
        out_ref[k, pl.ds(pl.multiple_of(h * rows, 8), rows)] = acc[h, k]

    def finish(k):
        swap(k).wait()
        exponent = swap_in[k, 0:EXPONENT_ROWS].astype(jnp.int32).astype(F32)[0:1]
        scale = jnp.broadcast_to(jnp.exp2(exponent - 14.9), (16, 2 * ny))

        @pl.loop(0, rows // 16)
        def _(r):
            g = swap_in[k, pl.ds(pl.multiple_of(EXPONENT_ROWS + r * 16, 16), 16)].astype(jnp.int32).astype(F32)
            out_ref[k, pl.ds(pl.multiple_of((1 - h) * rows + r * 16, 8), 16)] = g * scale

    for n in range(8):
        if n < 5:
            forward_y(n)
        if 1 <= n < 6:
            forward_x(n - 1)
        if 2 <= n < 7:
            gather(n - 2)
        if 3 <= n:
            finish(n - 3)

    for k in range(5):
        pl.when(not_self)(lambda: outgoing(0, k).wait_send())
        for i in range(1, shots):
            outgoing(i, k).wait_send()
        for i in range(1, half):
            hop_z(k, i).wait_send()
        for i in range(half):
            stays, moves, go, stay = hop_y(k, i)
            pl.when(moves)(go.wait_send)
        for i in range(8):
            stays, moves, go, stay = hop_x(k, i)
            pl.when(moves)(go.wait_send)


def y_matrix(ny):
    matrix = [[0.0] * (2 * ny) for _ in range(ny)]
    for y in range(ny):
        for k in range(1, 5):
            if y + k < ny:
                matrix[y + k][y] = FIRST[k - 1]
                matrix[y + k][ny + y] = SECOND[k - 1]
            if y - k >= 0:
                matrix[y - k][y] = -FIRST[k - 1]
                matrix[y - k][ny + y] = SECOND[k - 1]
    one = jnp.asarray(matrix, F32).astype(BF16)
    return jnp.concatenate([one, one], axis=0)


def on_device(velocity, epsilon, delta, tilt, azimuth, offsets, sources, traces, adjoint_state, snapshots):
    shots = lax.axis_size("shot")
    slabs = lax.axis_size("slab")
    half = slabs // 2
    _, _, nz, nx, ny = adjoint_state.shape
    nt = snapshots.shape[0]
    depth, width, lanes = velocity.shape
    rows = depth * width // 2
    tiles = nx // 16
    vmem = pl.BlockSpec(memory_space=pltpu.VMEM)
    smem = pl.BlockSpec(memory_space=pltpu.SMEM)
    hbm = pl.BlockSpec(memory_space=pl.ANY)
    dma = pltpu.SemaphoreType.DMA
    params = [m.reshape(depth * width, lanes) for m in (velocity, epsilon, delta, tilt, azimuth)]
    state = adjoint_state.reshape(4, nz, nx, ny)
    frames = snapshots.reshape(nt, 2, nz, nx, ny)
    coded = (8, EXPONENT_ROWS + 5 * rows, ny)
    final, gradients = pl.pallas_call(
        whole_kernel,
        out_shape=(
            jax.ShapeDtypeStruct((2, nz, nx, ny), F32),
            jax.ShapeDtypeStruct((5, 2 * rows, lanes), F32),
        ),
        in_specs=[vmem] * 5 + [smem] * 3 + [hbm, hbm, vmem],
        out_specs=(vmem, vmem),
        scratch_shapes=[
            pltpu.VMEM((2, 5, rows, lanes), BF16),
            pltpu.VMEM((shots, 5, rows, ny), BF16),
            pltpu.VMEM((half, 5, rows, ny), BF16),
            pltpu.VMEM((2, 2, nz + 8, nx + 16, ny), F32),
            pltpu.VMEM((2, nz, nx + 16, ny), F32),
            pltpu.VMEM((2, 2, nz, nx + 16, ny), F32),
            pltpu.VMEM((2, nz, nx, ny), F32),
            pltpu.VMEM((2, 2, nz, nx, ny), F32),
            pltpu.VMEM((tiles, 2 * nz * 16, ny), F32),
            pltpu.VMEM((tiles, 2 * nz * 16, 2 * ny), BF16),
            pltpu.VMEM((tiles, 2 * nz * 16, 2 * ny), BF16),
            pltpu.VMEM((9, nz, nx, ny), F32),
            pltpu.VMEM((8, nz, nx, ny), F32),
            pltpu.VMEM((5, nz, nx, ny), F32),
            pltpu.VMEM((nz, 2 * nx, ny), F32),
            pltpu.VMEM((nt, 2, nz, nx, ny), BF16),
            pltpu.VMEM((5, nx, ny), F32),
            pltpu.VMEM(coded, jnp.int16),
            pltpu.VMEM(coded, jnp.int16),
            pltpu.VMEM(coded, jnp.int16),
            pltpu.VMEM(coded, jnp.int16),
            pltpu.VMEM((2, 5, rows, lanes), F32),
            pltpu.VMEM((5, EXPONENT_ROWS + rows, lanes), jnp.int16),
            pltpu.VMEM((5, EXPONENT_ROWS + rows, lanes), jnp.int16),
            dma((5,)), dma((5,)), dma((5,)), dma((shots, 5)), dma((half, 5)), dma((5,)),
            dma((2, 2, tiles)), dma((2, 2, tiles)),
            dma((3, 5, 8)), dma((3, 5, 8)), dma((5, 5)), dma((5,)), dma((5,)),
        ],
        compiler_params=pltpu.CompilerParams(collective_id=0, has_side_effects=True, vmem_limit_bytes=VMEM_LIMIT),
        name="whole",
    )(*params, offsets.T, sources, traces, state, frames, y_matrix(ny))
    return (gradients.reshape(5, depth, width, lanes), final.reshape(2, 1, nz, nx, ny))


def solution(mesh):
    return jax.shard_map(
        on_device,
        mesh=mesh,
        in_specs=(
            P("shot", "slab", None),
            P("shot", "slab", None),
            P("shot", "slab", None),
            P("shot", "slab", None),
            P("shot", "slab", None),
            P(),
            P("shot"),
            P("shot", None),
            P(None, "shot", "slab", None, None),
            P(None, None, "shot", "slab", None, None),
        ),
        out_specs=(P(None, "shot", "slab", None), P(None, "shot", "slab", None, None)),
        check_vma=False,
    )
```

```python
import functools
import jax
import jax.numpy as jnp
from jax import lax
from jax.sharding import PartitionSpec as P
from jax.experimental import pallas as pl
from jax.experimental.pallas import tpu as pltpu

MESH = pl.DeviceIdType.MESH
F32 = jnp.float32
BF16 = jnp.bfloat16

SECOND = (63.0, -7.875, 1.0, -9.0 / 128.0)
FIRST = (21.0, -5.25, 1.0, -3.0 / 32.0)
UNIT2 = 8.0 / 315.0
UNIT11 = (4.0 / 105.0) ** 2
CENTRE = -7175.0 / 64.0
EXPONENT_ROWS = 16
CHUNKS = ((0,), (1, 2), (3, 4))
VMEM_LIMIT = 60 * 1024 * 1024


def second(at):
    total = at(3) + at(-3)
    for k in (1, 2, 4):
        total = total + SECOND[k - 1] * (at(k) + at(-k))
    return total


def first(at):
    total = at(3) - at(-3)
    for k in (1, 2, 4):
        total = total + FIRST[k - 1] * (at(k) - at(-k))
    return total


def sine_cosine(angle):
    u = 0.5 * angle
    w = u * u
    s = 1.0 / 362880.0 - w * (1.0 / 39916800.0)
    for term in (-1.0 / 5040.0, 1.0 / 120.0, -1.0 / 6.0, 1.0):
        s = term + w * s
    s = s * u
    c = -1.0 / 3628800.0 + w * (1.0 / 479001600.0)
    for term in (1.0 / 40320.0, -1.0 / 720.0, 1.0 / 24.0, -0.5, 1.0):
        c = term + w * c
    return 2.0 * s * c, 1.0 - 2.0 * s * s


def where_am_i():
    me_s = lax.axis_index("shot")
    me_b = lax.axis_index("slab")
    half = lax.axis_size("slab") // 2
    return me_s, me_b, half, me_b // half, lax.rem(me_b, half)


def remote(source, target, send, recv, device):
    return pltpu.make_async_remote_copy(
        src_ref=source, dst_ref=target, send_sem=send, recv_sem=recv, device_id=device, device_id_type=MESH)


def whole_kernel(v_ref, e_ref, d_ref, t_ref, a_ref, offsets_ref, sources_ref, traces_ref, state_ref, snap_hbm, y1_ref,
                 final_ref, out_ref,
                 both, sendbuf, pin, F, GZ, GY, ZZ, YY, ZY, SF, SG, COEF, ACC, TRIG, dbl, SNAP, MX,
                 GQ, first_in, second_in, third_in, acc, swap_out, swap_in,
                 in_sem, psend, precv, asend, arecv, aloc, hsend, hrecv, rsend, rrecv, rloc, ssend, srecv):
    me_s, me_b, half, h, j_me = where_am_i()
    shots = lax.axis_size("shot")
    slabs = 2 * half
    nz, nx, ny = state_ref.shape[1:]
    nt = SNAP.shape[0]
    tiles = nx // 16
    rows = nz * 8
    block = 2 * nz * 16
    partner = (me_s, lax.rem(me_b + half, slabs))
    x, y_hi, y_lo = me_s // 2, lax.rem(me_s, 2), h
    y_me = y_hi * 2 + y_lo
    columns = shots // 2

    target = 2 * me_s + h
    src_s, src_h = me_b // 2, lax.rem(me_b, 2)
    is_self = target == me_b
    not_self = target != me_b
    has_up = me_b > 0
    has_down = me_b < slabs - 1
    up = (me_s, lax.max(me_b - 1, 0))
    down = (me_s, lax.min(me_b + 1, slabs - 1))

    def z_line(i):
        return (me_s, y_lo * half + lax.rem(j_me + i, half))

    def y_line(i):
        y = lax.rem(y_me + i, 4)
        return (x * 2 + y // 2, lax.rem(y, 2) * half + j_me)

    def x_line(i):
        return (lax.rem(x + i, columns) * 2 + y_hi, me_b)

    barrier = pltpu.get_barrier_semaphore()

    def greet(device):
        pl.semaphore_signal(barrier, inc=1, device_id=device, device_id_type=MESH)

    for i in range(1, half):
        greet(z_line(i))
    for i in range(1, 4):
        greet(y_line(i))
    for i in range(1, columns):
        greet(x_line(i))
    pl.when(has_up)(lambda: greet(up))
    pl.when(has_down)(lambda: greet(down))
    for j in range(half):
        pl.when((src_s != me_s) | (src_h * half + j != me_b))(lambda: greet((src_s, src_h * half + j)))

    loads = [pltpu.make_async_copy(state_ref.at[n], F.at[n // 2, n % 2, pl.ds(4, nz), pl.ds(8, nx)], in_sem.at[n])
             for n in range(4)]
    loads.append(pltpu.make_async_copy(snap_hbm, SNAP, in_sem.at[4]))
    for c in loads:
        c.start()

    @pl.loop(0, nz + 8)
    def _(z):
        for slot in range(2):
            for f in range(2):
                F[slot, f, z, 0:8] = jnp.zeros((8, ny), F32)
                F[slot, f, z, 8 + nx:16 + nx] = jnp.zeros((8, ny), F32)

    @pl.loop(0, nz)
    def _(z):
        for f in range(2):
            for g in (GZ, GY):
                g[f, z, 0:8] = jnp.zeros((8, ny), F32)
                g[f, z, 8 + nx:16 + nx] = jnp.zeros((8, ny), F32)

    def clear(first_row):
        @pl.loop(0, 4)
        def _(z):
            for slot in range(2):
                for f in range(2):
                    F[slot, f, first_row + z] = jnp.zeros((nx + 16, ny), F32)

    pl.when(me_b == 0)(lambda: clear(0))
    pl.when(me_b == slabs - 1)(lambda: clear(nz + 4))

    pl.semaphore_wait(barrier, (half - 1) + 3 + (columns - 1) + has_up.astype(jnp.int32) + has_down.astype(jnp.int32)
                      + shots - is_self.astype(jnp.int32))

    params = (v_ref, e_ref, d_ref, t_ref, a_ref)
    theirs = pl.ds(pl.multiple_of(rows * (1 - h), 16), rows)
    ours = pl.ds(pl.multiple_of(rows * h, 16), rows)
    swaps = [remote(params[k].at[theirs], both.at[h, k], psend.at[k], precv.at[k], partner) for k in range(5)]
    for c in swaps:
        c.start()
    for k in range(5):
        both[h, k] = params[k][ours]

    def halo(slot, direction, q):
        rows = (pl.ds(4, 4), pl.ds(nz + 4, 4)) if direction == 0 else (pl.ds(nz, 4), pl.ds(0, 4))
        return remote(F.at[slot, :, rows[0], pl.ds(8 + 16 * q, 16)], F.at[slot, :, rows[1], pl.ds(8 + 16 * q, 16)],
                      hsend.at[slot, direction, q], hrecv.at[slot, direction, q], (up, down)[direction])

    def send_halos(slot, q, direction):
        pl.when((has_up, has_down)[direction])(lambda: halo(slot, direction, q).start())

    def wait_halos(slot, q):
        @pl.when(has_up)
        def _():
            halo(slot, 0, q).wait_send()
            halo(slot, 1, q).wait_recv()

        @pl.when(has_down)
        def _():
            halo(slot, 1, q).wait_send()
            halo(slot, 0, q).wait_recv()

    row_id = lax.broadcasted_iota(jnp.int32, (16, 128), 0)
    residue = j_me * 8 + lax.rem(row_id, 8)
    lane = lax.broadcasted_iota(jnp.int32, (16, 128), 1)

    def outgoing(i, k):
        s = lax.rem(me_s + i, shots)
        return remote(sendbuf.at[i, k], pin.at[j_me, k], asend.at[i, k], arecv.at[j_me, k], (s, target))

    def local(k):
        return pltpu.make_async_copy(sendbuf.at[0, k], pin.at[j_me, k], aloc.at[k])

    for k in range(5):
        swaps[k].wait()

        @pl.loop(0, rows // 16)
        def _(r):
            at = pl.ds(pl.multiple_of(r * 16, 16), 16)
            lo = both[0, k, at].astype(F32)
            hi = both[1, k, at].astype(F32)
            for i in range(shots):
                s = lax.rem(me_s + i, shots)
                upper = residue < offsets_ref[0, s]
                right = lane < offsets_ref[1, s]
                left_part = jnp.where(upper, hi[:, :128], lo[:, :128])
                right_part = jnp.where(upper, hi[:, 128:], lo[:, 128:])
                sendbuf[i, k, at] = jnp.where(right, right_part, left_part).astype(BF16)
        pl.when(not_self)(lambda: outgoing(0, k).start())
        pl.when(is_self)(lambda: local(k).start())
        for i in range(1, shots):
            outgoing(i, k).start()

    for c in loads[:4]:
        c.wait()
    for q in range(tiles):
        send_halos(0, q, 0)
        send_halos(0, q, 1)

    def split(value, store):
        hi = value.astype(BF16)
        store(slice(0, ny), hi)
        store(slice(ny, 2 * ny), (value - hi.astype(F32)).astype(BF16))

    def along_y(q):
        out = jnp.dot(SF[q], y1_ref[...], preferred_element_type=F32)
        for f in range(2):
            for z in range(nz):
                at = (f * nz + z) * 16
                GY[f, z, 8 + 16 * q:24 + 16 * q] = out[at:at + 16, 0:ny]
                YY[f, z, 16 * q:16 * q + 16] = out[at:at + 16, ny:2 * ny]

    for q in range(tiles):
        for f in range(2):
            @pl.loop(0, nz)
            def _(z):
                at = pl.ds(pl.multiple_of((f * nz + z) * 16, 16), 16)

                def store(lanes, value):
                    SF[q, at, lanes] = value
                split(F[0, f, z + 4, 8 + 16 * q:24 + 16 * q], store)

    ox = lax.rem(offsets_ref[0, me_s], nx)
    oy = lax.rem(offsets_ref[1, me_s], ny)
    lane_shift = lax.rem(ny - oy, ny)
    for k in range(5):
        for j in range(half):
            here = is_self & (j_me == j)
            away = not_self | (j_me != j)
            pl.when(here)(lambda: local(k).wait())
            pl.when(away)(lambda: remote(sendbuf.at[0, k], pin.at[j, k], asend.at[0, k], arecv.at[j, k],
                                         (src_s, src_h * half + j)).wait_recv())

        @pl.loop(0, nz // 2)
        def _(zz):
            for j in range(half):
                two = pin[j, k, pl.ds(pl.multiple_of(zz * 16, 16), 16)].astype(F32)
                for half_row in range(2):
                    part = two[8 * half_row:8 * half_row + 8]
                    dbl[zz * 2 + half_row, 8 * j:8 * j + 8] = part
                    dbl[zz * 2 + half_row, nx + 8 * j:nx + 8 * j + 8] = part

        @pl.loop(0, nz)
        def _(z):
            TRIG[k, z] = pltpu.roll(dbl[z, pl.ds(ox, nx)], lane_shift, 1)

    source = sources_ref[0]
    first_row = me_b * nz

    @pl.loop(0, nz)
    def _(z):
        for t in range(tiles):
            at = pl.ds(16 * t, 16)
            v = TRIG[0, z, at]
            c = v * v
            a = 1.0 + 2.0 * TRIG[1, z, at]
            b = jnp.sqrt(1.0 + 2.0 * TRIG[2, z, at])
            st, ct = sine_cosine(TRIG[3, z, at])
            sa, ca = sine_cosine(TRIG[4, z, at])
            n_z, n_x, n_y = ct, st * ca, st * sa
            TRIG[1, z, at] = st
            TRIG[2, z, at] = ct
            TRIG[3, z, at] = sa
            TRIG[4, z, at] = ca
            mixed = 2.0 * UNIT11 / UNIT2
            COEF[0, z, at] = n_z * n_z
            COEF[1, z, at] = n_x * n_x
            COEF[2, z, at] = mixed * n_z * n_x
            COEF[3, z, at] = mixed * n_z * n_y
            COEF[4, z, at] = mixed * n_x * n_y
            COEF[5, z, at] = a
            COEF[6, z, at] = b
            COEF[7, z, at] = UNIT2 * c
            cell = (((first_row + z) * nx + 16 * t + lax.broadcasted_iota(jnp.int32, (16, ny), 0)) * ny
                    + lax.broadcasted_iota(jnp.int32, (16, ny), 1))
            COEF[8, z, at] = jnp.where(cell == source, c, 0.0)
            for n in range(8):
                ACC[n, z, at] = jnp.zeros((16, ny), F32)

    loads[4].wait()

    def depth_pass(cur, q):
        for f in range(2):
            row = [F[cur, f, z, 8 + 16 * q:24 + 16 * q] for z in range(nz + 8)]
            for z in range(nz):
                ZZ[f, z, 16 * q:16 * q + 16] = second(lambda k: row[z + 4 + k])
                g = first(lambda k: row[z + 4 + k])
                GZ[f, z, 8 + 16 * q:24 + 16 * q] = g
                at = (f * nz + z) * 16

                def store(lanes, value):
                    SG[q, at:at + 16, lanes] = value
                split(g, store)

    def update(t, cur, nxt, q, z, amplitude):
        at = pl.ds(16 * q, 16)
        inner = pl.ds(8 + 16 * q, 16)

        def parts(f):
            def x_of(ref, *lead):
                return lambda k: ref[(*lead, pl.ds(8 + 16 * q + k, 16))]
            yy = YY[f, z, at]
            return (
                ZZ[f, z, at] - yy,
                second(x_of(F, cur, f, z + 4)) - yy,
                first(x_of(GZ, f, z)),
                ZY[q, pl.ds(pl.multiple_of((f * nz + z) * 16, 16), 16)],
                first(x_of(GY, f, z)),
                yy,
                F[cur, f, z + 4, inner],
            )
        coef = [COEF[n, z, at] for n in range(5)]
        dp = parts(0)
        dq = parts(1)

        def weighted(d):
            total = coef[0] * d[0]
            for n in range(1, 5):
                total = total + coef[n] * d[n]
            return total
        base_p = dp[5] + CENTRE * dp[6]
        base_q = dq[5] + CENTRE * dq[6]
        h2 = (dp[0] + dp[1]) + (base_p + base_p) - weighted(dp)
        h1 = base_q + weighted(dq)
        a = COEF[5, z, at]
        b = COEF[6, z, at]
        c = COEF[7, z, at]
        pn = (dp[6] + dp[6]) - F[nxt, 0, z + 4, inner] + c * (a * h2 + b * h1)
        pn = pn + amplitude * COEF[8, z, at]
        qn = (dq[6] + dq[6]) - F[nxt, 1, z + 4, inner] + c * (b * h2 + h1)
        F[nxt, 0, z + 4, inner] = pn
        F[nxt, 1, z + 4, inner] = qn
        for f, value in ((0, pn), (1, qn)):
            def store(lanes, part):
                SF[q, pl.ds(pl.multiple_of((f * nz + z) * 16, 16), 16), lanes] = part
            split(value, store)
        pf = SNAP[t, 0, z, at].astype(F32)
        qf = SNAP[t, 1, z, at].astype(F32)
        bp = b * pf
        wa = a * pf + b * qf
        wb = bp + qf
        ACC[0, z, at] += h2 * wa + h1 * wb
        ACC[1, z, at] += h2 * pf
        ACC[2, z, at] += h1 * pf + h2 * qf
        for n in range(5):
            ACC[3 + n, z, at] += dq[n] * wb - dp[n] * wa

    def step(t, carry):
        cur = lax.rem(t, 2)
        nxt = 1 - cur
        amplitude = traces_ref[0, t]
        along_y(0)
        wait_halos(cur, 0)
        depth_pass(cur, 0)
        for q in range(tiles):
            if q + 1 < tiles:
                wait_halos(cur, q + 1)
                depth_pass(cur, q + 1)
                along_y(q + 1)
            ZY[q] = jnp.dot(SG[q], y1_ref[:, 0:ny], preferred_element_type=F32)
            for direction in range(2):
                for z in range(4):
                    update(t, cur, nxt, q, 8 * direction + z, amplitude)
                pl.when(t < nt - 1)(lambda: send_halos(nxt, q, direction))
        for q in range(tiles):
            @pl.loop(4, 8, step=4)
            def _(z0):
                for z in range(4):
                    update(t, cur, nxt, q, z0 + z, amplitude)
        return carry

    lax.fori_loop(0, nt, step, 0)
    last = nt % 2
    for f in range(2):
        @pl.loop(0, nz)
        def _(z):
            final_ref[f, z] = F[last, f, z + 4, 8:8 + nx]

    back_shift = lax.rem(nx - ox, nx)
    MX[...] = jnp.zeros_like(MX)

    @pl.loop(0, nz)
    def _(z):
        v = TRIG[0, z]
        st, ct, sa, ca = (TRIG[n, z] for n in range(1, 5))
        c = v * v
        b = COEF[6, z]
        n_z, n_x, n_y = ct, st * ca, st * sa
        g = [ACC[n, z] for n in range(8)]
        t_z, t_x, t_y = -st, ct * ca, ct * sa
        a_x, a_y = -st * sa, st * ca
        r = UNIT11 / UNIT2
        tilt = (t_z * n_z * g[3] + t_x * n_x * g[4]
                + r * ((t_z * n_x + t_x * n_z) * g[5] + (t_z * n_y + t_y * n_z) * g[6]
                       + (t_x * n_y + t_y * n_x) * g[7]))
        turn = (a_x * n_x * g[4]
                + r * (a_x * n_z * g[5] + a_y * n_z * g[6] + (a_x * n_y + a_y * n_x) * g[7]))
        sums = (
            2.0 * UNIT2 * v * g[0],
            2.0 * UNIT2 * c * g[1],
            UNIT2 * (c / b) * g[2],
            2.0 * UNIT2 * c * tilt,
            2.0 * UNIT2 * c * turn,
        )
        for k in range(5):
            for part in range(2):
                dbl[k, part * nx:(part + 1) * nx] = sums[k]
        for k in range(5):
            value = pltpu.roll(dbl[k, pl.ds(back_shift, nx)], oy, 1)
            TRIG[k, z] = value
            MX[k] = jnp.maximum(MX[k], jnp.abs(value))

    def exponent_of(largest):
        return jnp.ceil(jnp.log2(jnp.maximum(jnp.max(largest, axis=0, keepdims=True), 1e-30)))

    def exponent_rows(exponents):
        rest = [jnp.zeros_like(exponents[0])] * (EXPONENT_ROWS - len(exponents))
        return jnp.concatenate(exponents + rest, axis=0).astype(jnp.int32).astype(jnp.int16)

    def coded(value):
        return jnp.round(value).astype(jnp.int32).astype(jnp.int16)

    for j in range(half):
        exponents = []
        for k in range(5):
            exponents.append(exponent_of(MX[k, 8 * j:8 * j + 8]))
            MX[k, 8 * j:8 * j + 8] = jnp.broadcast_to(jnp.exp2(14.9 - exponents[k]), (8, ny))
        GQ[j, 0:EXPONENT_ROWS] = exponent_rows(exponents)

    def chunk(n):
        begin = EXPONENT_ROWS + CHUNKS[n][0] * rows if n else 0
        return pl.ds(begin, EXPONENT_ROWS + (CHUNKS[n][-1] + 1) * rows - begin)

    def hop_z(k, i):
        j = lax.rem(j_me + i, half)
        return remote(GQ.at[j, chunk(k)], first_in.at[j_me, chunk(k)], rsend.at[0, k, j], rrecv.at[0, k, j_me],
                      (me_s, y_lo * half + j))

    def own_z(k):
        return pltpu.make_async_copy(GQ.at[j_me, chunk(k)], first_in.at[j_me, chunk(k)], rloc.at[k, 0])

    for n, members in enumerate(CHUNKS):
        for k in members:
            @pl.loop(0, nz // 2)
            def _(zz):
                for j in range(half):
                    scale = MX[k, 8 * j:8 * j + 8]
                    pair = jnp.concatenate([TRIG[k, 2 * zz, 8 * j:8 * j + 8] * scale,
                                            TRIG[k, 2 * zz + 1, 8 * j:8 * j + 8] * scale], axis=0)
                    GQ[j, pl.ds(pl.multiple_of(EXPONENT_ROWS + k * rows + zz * 16, 16), 16)] = coded(pair)
        own_z(n).start()
        for i in range(1, half):
            hop_z(n, i).start()

    def hop_y(k, i):
        j = lax.rem(j_me + i, half)
        z1, z0, c = j // 4, lax.rem(j // 2, 2), lax.rem(j, 2)
        slot = y_me * 2 + z1
        go = remote(first_in.at[j, chunk(k)], second_in.at[slot, chunk(k)], rsend.at[1, k, j], rrecv.at[1, k, slot],
                    (x * 2 + z0, c * half + j_me))
        stay = pltpu.make_async_copy(first_in.at[j, chunk(k)], second_in.at[slot, chunk(k)], rloc.at[k, 1 + z1])
        return (z0 == y_hi) & (c == y_lo), (z0 != y_hi) | (c != y_lo), go, stay

    def forward_y(k):
        for i in range(half):
            j = lax.rem(j_me + i, half)
            if i == 0:
                own_z(k).wait()
            else:
                remote(GQ.at[j, chunk(k)], first_in.at[j, chunk(k)], rsend.at[0, k, j], rrecv.at[0, k, j],
                       (me_s, y_lo * half + j)).wait_recv()
            stays, moves, go, stay = hop_y(k, i)
            pl.when(moves)(go.start)
            pl.when(stays)(stay.start)

    def hop_x(k, i):
        slot = lax.rem(y_me * 2 + i, 8)
        from_hi, from_lo, z1 = slot // 4, lax.rem(slot // 2, 2), lax.rem(slot, 2)
        to_x = 2 * from_lo + z1
        shot = x * 2 + from_hi
        go = remote(second_in.at[slot, chunk(k)], third_in.at[shot, chunk(k)], rsend.at[2, k, slot],
                    rrecv.at[2, k, shot], (to_x * 2 + y_hi, me_b))
        stay = pltpu.make_async_copy(second_in.at[slot, chunk(k)], third_in.at[shot, chunk(k)],
                                     rloc.at[k, 3 + from_hi])
        return to_x == x, to_x != x, go, stay

    def forward_x(k):
        for i in range(8):
            slot = lax.rem(y_me * 2 + i, 8)
            if i < 2:
                pltpu.make_async_copy(first_in.at[0, chunk(k)], second_in.at[slot, chunk(k)], rloc.at[k, 1 + i]).wait()
            else:
                from_hi, from_lo = slot // 4, lax.rem(slot // 2, 2)
                remote(first_in.at[0, chunk(k)], second_in.at[slot, chunk(k)], rsend.at[1, k, 0],
                       rrecv.at[1, k, slot], (x * 2 + from_hi, from_lo * half + j_me)).wait_recv()
            stays, moves, go, stay = hop_x(k, i)
            pl.when(moves)(go.start)
            pl.when(stays)(stay.start)

    def swap(k):
        return remote(swap_out.at[k], swap_in.at[k], ssend.at[k], srecv.at[k], partner)

    def arrive(k):
        for i in range(shots):
            s = lax.rem(me_s + i, shots)
            here = s // 2 == x
            away = s // 2 != x
            pl.when(here)(lambda: pltpu.make_async_copy(
                second_in.at[0, chunk(k)], third_in.at[s, chunk(k)], rloc.at[k, 3 + lax.rem(s, 2)]).wait())
            pl.when(away)(lambda: remote(
                second_in.at[0, chunk(k)], third_in.at[s, chunk(k)], rsend.at[2, k, 0], rrecv.at[2, k, s],
                (s // 2 * 2 + y_hi, me_b)).wait_recv())

    def gather(k):
        scales = []
        for s in range(shots):
            exponents = third_in[s, 0:EXPONENT_ROWS].astype(jnp.int32).astype(F32)
            scales.append(jnp.broadcast_to(jnp.exp2(exponents[k:k + 1] - 14.9), (16, 128)))

        @pl.loop(0, rows // 16)
        def _(r):
            at = pl.ds(pl.multiple_of(r * 16, 16), 16)
            total = [[0.0, 0.0], [0.0, 0.0]]
            for s in range(shots):
                upper = residue < offsets_ref[0, s]
                right = lane < offsets_ref[1, s]
                g = third_in[s, pl.ds(pl.multiple_of(EXPONENT_ROWS + k * rows + r * 16, 16), 16)]
                g = g.astype(jnp.int32).astype(F32) * scales[s]
                hi = jnp.where(upper, g, 0.0)
                for c, part in ((0, g - hi), (1, hi)):
                    right_part = jnp.where(right, part, 0.0)
                    total[c][1] = total[c][1] + right_part
                    total[c][0] = total[c][0] + (part - right_part)
            for c in range(2):
                acc[c, k, at, 0:128] = total[c][0]
                acc[c, k, at, 128:256] = total[c][1]
        largest = jnp.abs(acc[1 - h, k, 0:8])
        for r in range(1, rows // 8):
            largest = jnp.maximum(largest, jnp.abs(acc[1 - h, k, 8 * r:8 * r + 8]))
        exponent = exponent_of(largest)
        swap_out[k, 0:EXPONENT_ROWS] = exponent_rows([exponent])
        scale = jnp.broadcast_to(jnp.exp2(14.9 - exponent), (16, 2 * ny))

        @pl.loop(0, rows // 16)
        def _(r):
            at = pl.ds(pl.multiple_of(r * 16, 16), 16)
            swap_out[k, pl.ds(pl.multiple_of(EXPONENT_ROWS + r * 16, 16), 16)] = coded(acc[1 - h, k, at] * scale)
        swap(k).start()
        out_ref[k, pl.ds(pl.multiple_of(h * rows, 8), rows)] = acc[h, k]

    def finish(k):
        swap(k).wait()
        exponent = swap_in[k, 0:EXPONENT_ROWS].astype(jnp.int32).astype(F32)[0:1]
        scale = jnp.broadcast_to(jnp.exp2(exponent - 14.9), (16, 2 * ny))

        @pl.loop(0, rows // 16)
        def _(r):
            g = swap_in[k, pl.ds(pl.multiple_of(EXPONENT_ROWS + r * 16, 16), 16)].astype(jnp.int32).astype(F32)
            out_ref[k, pl.ds(pl.multiple_of((1 - h) * rows + r * 16, 8), 16)] = g * scale

    for n in range(len(CHUNKS) + 2):
        if n < len(CHUNKS):
            forward_y(n)
        if 1 <= n < len(CHUNKS) + 1:
            forward_x(n - 1)
        if 2 <= n:
            arrive(n - 2)
            for k in CHUNKS[n - 2]:
                gather(k)
    for k in range(5):
        finish(k)

    for k in range(5):
        pl.when(not_self)(lambda: outgoing(0, k).wait_send())
        for i in range(1, shots):
            outgoing(i, k).wait_send()
    for n in range(len(CHUNKS)):
        for i in range(1, half):
            hop_z(n, i).wait_send()
        for i in range(half):
            stays, moves, go, stay = hop_y(n, i)
            pl.when(moves)(go.wait_send)
        for i in range(8):
            stays, moves, go, stay = hop_x(n, i)
            pl.when(moves)(go.wait_send)


def y_matrix(ny):
    matrix = [[0.0] * (2 * ny) for _ in range(ny)]
    for y in range(ny):
        for k in range(1, 5):
            if y + k < ny:
                matrix[y + k][y] = FIRST[k - 1]
                matrix[y + k][ny + y] = SECOND[k - 1]
            if y - k >= 0:
                matrix[y - k][y] = -FIRST[k - 1]
                matrix[y - k][ny + y] = SECOND[k - 1]
    one = jnp.asarray(matrix, F32).astype(BF16)
    return jnp.concatenate([one, one], axis=0)


def on_device(velocity, epsilon, delta, tilt, azimuth, offsets, sources, traces, adjoint_state, snapshots):
    shots = lax.axis_size("shot")
    slabs = lax.axis_size("slab")
    half = slabs // 2
    _, _, nz, nx, ny = adjoint_state.shape
    nt = snapshots.shape[0]
    depth, width, lanes = velocity.shape
    rows = depth * width // 2
    tiles = nx // 16
    vmem = pl.BlockSpec(memory_space=pltpu.VMEM)
    smem = pl.BlockSpec(memory_space=pltpu.SMEM)
    hbm = pl.BlockSpec(memory_space=pl.ANY)
    dma = pltpu.SemaphoreType.DMA
    params = [m.reshape(depth * width, lanes) for m in (velocity, epsilon, delta, tilt, azimuth)]
    state = adjoint_state.reshape(4, nz, nx, ny)
    frames = snapshots.reshape(nt, 2, nz, nx, ny)
    coded = (8, EXPONENT_ROWS + 5 * rows, ny)
    final, gradients = pl.pallas_call(
        whole_kernel,
        out_shape=(
            jax.ShapeDtypeStruct((2, nz, nx, ny), F32),
            jax.ShapeDtypeStruct((5, 2 * rows, lanes), F32),
        ),
        in_specs=[vmem] * 5 + [smem] * 3 + [hbm, hbm, vmem],
        out_specs=(vmem, vmem),
        scratch_shapes=[
            pltpu.VMEM((2, 5, rows, lanes), BF16),
            pltpu.VMEM((shots, 5, rows, ny), BF16),
            pltpu.VMEM((half, 5, rows, ny), BF16),
            pltpu.VMEM((2, 2, nz + 8, nx + 16, ny), F32),
            pltpu.VMEM((2, nz, nx + 16, ny), F32),
            pltpu.VMEM((2, nz, nx + 16, ny), F32),
            pltpu.VMEM((2, nz, nx, ny), F32),
            pltpu.VMEM((2, nz, nx, ny), F32),
            pltpu.VMEM((tiles, 2 * nz * 16, ny), F32),
            pltpu.VMEM((tiles, 2 * nz * 16, 2 * ny), BF16),
            pltpu.VMEM((tiles, 2 * nz * 16, 2 * ny), BF16),
            pltpu.VMEM((9, nz, nx, ny), F32),
            pltpu.VMEM((8, nz, nx, ny), F32),
            pltpu.VMEM((5, nz, nx, ny), F32),
            pltpu.VMEM((nz, 2 * nx, ny), F32),
            pltpu.VMEM((nt, 2, nz, nx, ny), BF16),
            pltpu.VMEM((5, nx, ny), F32),
            pltpu.VMEM(coded, jnp.int16),
            pltpu.VMEM(coded, jnp.int16),
            pltpu.VMEM(coded, jnp.int16),
            pltpu.VMEM(coded, jnp.int16),
            pltpu.VMEM((2, 5, rows, lanes), F32),
            pltpu.VMEM((5, EXPONENT_ROWS + rows, lanes), jnp.int16),
            pltpu.VMEM((5, EXPONENT_ROWS + rows, lanes), jnp.int16),
            dma((5,)), dma((5,)), dma((5,)), dma((shots, 5)), dma((half, 5)), dma((5,)),
            dma((2, 2, tiles)), dma((2, 2, tiles)),
            dma((3, 5, 8)), dma((3, 5, 8)), dma((5, 5)), dma((5,)), dma((5,)),
        ],
        compiler_params=pltpu.CompilerParams(collective_id=0, has_side_effects=True, vmem_limit_bytes=VMEM_LIMIT),
        name="whole",
    )(*params, offsets.T, sources, traces, state, frames, y_matrix(ny))
    return (gradients.reshape(5, depth, width, lanes), final.reshape(2, 1, nz, nx, ny))


def solution(mesh):
    return jax.shard_map(
        on_device,
        mesh=mesh,
        in_specs=(
            P("shot", "slab", None),
            P("shot", "slab", None),
            P("shot", "slab", None),
            P("shot", "slab", None),
            P("shot", "slab", None),
            P(),
            P("shot"),
            P("shot", None),
            P(None, "shot", "slab", None, None),
            P(None, None, "shot", "slab", None, None),
        ),
        out_specs=(P(None, "shot", "slab", None), P(None, "shot", "slab", None, None)),
        check_vma=False,
    )
```

```python
import functools
import jax
import jax.numpy as jnp
from jax import lax
from jax.sharding import PartitionSpec as P
from jax.experimental import pallas as pl
from jax.experimental.pallas import tpu as pltpu

MESH = pl.DeviceIdType.MESH
F32 = jnp.float32
BF16 = jnp.bfloat16

SECOND = (63.0, -7.875, 1.0, -9.0 / 128.0)
FIRST = (21.0, -5.25, 1.0, -3.0 / 32.0)
UNIT2 = 8.0 / 315.0
UNIT11 = (4.0 / 105.0) ** 2
CENTRE = -7175.0 / 64.0
EXPONENT_ROWS = 16
CHUNKS = ((0,), (1, 2), (3, 4))
VMEM_LIMIT = 60 * 1024 * 1024


def second(at):
    total = at(3) + at(-3)
    for k in (1, 2, 4):
        total = total + SECOND[k - 1] * (at(k) + at(-k))
    return total


def first(at):
    total = at(3) - at(-3)
    for k in (1, 2, 4):
        total = total + FIRST[k - 1] * (at(k) - at(-k))
    return total


def sine_cosine(angle):
    u = 0.5 * angle
    w = u * u
    s = 1.0 / 362880.0 - w * (1.0 / 39916800.0)
    for term in (-1.0 / 5040.0, 1.0 / 120.0, -1.0 / 6.0, 1.0):
        s = term + w * s
    s = s * u
    c = -1.0 / 3628800.0 + w * (1.0 / 479001600.0)
    for term in (1.0 / 40320.0, -1.0 / 720.0, 1.0 / 24.0, -0.5, 1.0):
        c = term + w * c
    return 2.0 * s * c, 1.0 - 2.0 * s * s


def where_am_i():
    me_s = lax.axis_index("shot")
    me_b = lax.axis_index("slab")
    half = lax.axis_size("slab") // 2
    return me_s, me_b, half, me_b // half, lax.rem(me_b, half)


def remote(source, target, send, recv, device):
    return pltpu.make_async_remote_copy(
        src_ref=source, dst_ref=target, send_sem=send, recv_sem=recv, device_id=device, device_id_type=MESH)


def whole_kernel(v_ref, e_ref, d_ref, t_ref, a_ref, offsets_ref, sources_ref, traces_ref, state_ref, snap_hbm, y1_ref,
                 final_ref, out_ref,
                 both, sendbuf, pin, F, GZ, GY, ZZ, YY, ZY, SF, SG, COEF, ACC, TRIG, dbl, SNAP, MX,
                 GQ, first_in, second_in, third_in, acc, swap_out, swap_in,
                 in_sem, psend, precv, asend, arecv, aloc, hsend, hrecv, rsend, rrecv, rloc, ssend, srecv):
    me_s, me_b, half, h, j_me = where_am_i()
    shots = lax.axis_size("shot")
    slabs = 2 * half
    nz, nx, ny = state_ref.shape[1:]
    nt = SNAP.shape[0]
    tiles = nx // 16
    rows = nz * 8
    block = 2 * nz * 16
    partner = (me_s, lax.rem(me_b + half, slabs))
    x, y_hi, y_lo = me_s // 2, lax.rem(me_s, 2), h
    y_me = y_hi * 2 + y_lo
    columns = shots // 2

    target = 2 * me_s + h
    src_s, src_h = me_b // 2, lax.rem(me_b, 2)
    is_self = target == me_b
    not_self = target != me_b
    has_up = me_b > 0
    has_down = me_b < slabs - 1
    up = (me_s, lax.max(me_b - 1, 0))
    down = (me_s, lax.min(me_b + 1, slabs - 1))

    def z_line(i):
        return (me_s, y_lo * half + lax.rem(j_me + i, half))

    def y_line(i):
        y = lax.rem(y_me + i, 4)
        return (x * 2 + y // 2, lax.rem(y, 2) * half + j_me)

    def x_line(i):
        return (lax.rem(x + i, columns) * 2 + y_hi, me_b)

    barrier = pltpu.get_barrier_semaphore()

    def greet(device):
        pl.semaphore_signal(barrier, inc=1, device_id=device, device_id_type=MESH)

    for i in range(1, half):
        greet(z_line(i))
    for i in range(1, 4):
        greet(y_line(i))
    for i in range(1, columns):
        greet(x_line(i))
    pl.when(has_up)(lambda: greet(up))
    pl.when(has_down)(lambda: greet(down))
    for j in range(half):
        pl.when((src_s != me_s) | (src_h * half + j != me_b))(lambda: greet((src_s, src_h * half + j)))

    loads = [pltpu.make_async_copy(state_ref.at[n], F.at[n // 2, n % 2, pl.ds(4, nz), pl.ds(8, nx)], in_sem.at[n])
             for n in range(4)]
    loads.append(pltpu.make_async_copy(snap_hbm, SNAP, in_sem.at[4]))
    for c in loads:
        c.start()

    @pl.loop(0, nz + 8)
    def _(z):
        for slot in range(2):
            for f in range(2):
                F[slot, f, z, 0:8] = jnp.zeros((8, ny), F32)
                F[slot, f, z, 8 + nx:16 + nx] = jnp.zeros((8, ny), F32)

    @pl.loop(0, nz)
    def _(z):
        for f in range(2):
            for g in (GZ, GY):
                g[f, z, 0:8] = jnp.zeros((8, ny), F32)
                g[f, z, 8 + nx:16 + nx] = jnp.zeros((8, ny), F32)

    def clear(first_row):
        @pl.loop(0, 4)
        def _(z):
            for slot in range(2):
                for f in range(2):
                    F[slot, f, first_row + z] = jnp.zeros((nx + 16, ny), F32)

    pl.when(me_b == 0)(lambda: clear(0))
    pl.when(me_b == slabs - 1)(lambda: clear(nz + 4))

    pl.semaphore_wait(barrier, (half - 1) + 3 + (columns - 1) + has_up.astype(jnp.int32) + has_down.astype(jnp.int32)
                      + shots - is_self.astype(jnp.int32))

    params = (v_ref, e_ref, d_ref, t_ref, a_ref)
    theirs = pl.ds(pl.multiple_of(rows * (1 - h), 16), rows)
    ours = pl.ds(pl.multiple_of(rows * h, 16), rows)
    swaps = [remote(params[k].at[theirs], both.at[h, k], psend.at[k], precv.at[k], partner) for k in range(5)]
    for c in swaps:
        c.start()
    for k in range(5):
        both[h, k] = params[k][ours]

    def halo(slot, direction, q):
        rows = (pl.ds(4, 4), pl.ds(nz + 4, 4)) if direction == 0 else (pl.ds(nz, 4), pl.ds(0, 4))
        return remote(F.at[slot, :, rows[0], pl.ds(8 + 16 * q, 16)], F.at[slot, :, rows[1], pl.ds(8 + 16 * q, 16)],
                      hsend.at[slot, direction, q], hrecv.at[slot, direction, q], (up, down)[direction])

    def send_halos(slot, q, direction):
        pl.when((has_up, has_down)[direction])(lambda: halo(slot, direction, q).start())

    def wait_halos(slot, q):
        @pl.when(has_up)
        def _():
            halo(slot, 0, q).wait_send()
            halo(slot, 1, q).wait_recv()

        @pl.when(has_down)
        def _():
            halo(slot, 1, q).wait_send()
            halo(slot, 0, q).wait_recv()

    row_id = lax.broadcasted_iota(jnp.int32, (16, 128), 0)
    residue = j_me * 8 + lax.rem(row_id, 8)
    lane = lax.broadcasted_iota(jnp.int32, (16, 128), 1)

    def outgoing(i, k):
        s = lax.rem(me_s + i, shots)
        return remote(sendbuf.at[i, k], pin.at[j_me, k], asend.at[i, k], arecv.at[j_me, k], (s, target))

    def local(k):
        return pltpu.make_async_copy(sendbuf.at[0, k], pin.at[j_me, k], aloc.at[k])

    for k in range(5):
        swaps[k].wait()

        @pl.loop(0, rows // 16)
        def _(r):
            at = pl.ds(pl.multiple_of(r * 16, 16), 16)
            lo = both[0, k, at].astype(F32)
            hi = both[1, k, at].astype(F32)
            for i in range(shots):
                s = lax.rem(me_s + i, shots)
                upper = residue < offsets_ref[0, s]
                right = lane < offsets_ref[1, s]
                left_part = jnp.where(upper, hi[:, :128], lo[:, :128])
                right_part = jnp.where(upper, hi[:, 128:], lo[:, 128:])
                sendbuf[i, k, at] = jnp.where(right, right_part, left_part).astype(BF16)
        pl.when(not_self)(lambda: outgoing(0, k).start())
        pl.when(is_self)(lambda: local(k).start())
        for i in range(1, shots):
            outgoing(i, k).start()

    for c in loads[:4]:
        c.wait()
    for q in range(tiles):
        send_halos(0, q, 0)
        send_halos(0, q, 1)

    def split(value, store):
        hi = value.astype(BF16)
        store(slice(0, ny), hi)
        store(slice(ny, 2 * ny), (value - hi.astype(F32)).astype(BF16))

    def along_y(q):
        out = jnp.dot(SF[q], y1_ref[...], preferred_element_type=F32)
        for f in range(2):
            for z in range(nz):
                at = (f * nz + z) * 16
                GY[f, z, 8 + 16 * q:24 + 16 * q] = out[at:at + 16, 0:ny]
                YY[f, z, 16 * q:16 * q + 16] = out[at:at + 16, ny:2 * ny]

    for q in range(tiles):
        for f in range(2):
            @pl.loop(0, nz)
            def _(z):
                at = pl.ds(pl.multiple_of((f * nz + z) * 16, 16), 16)

                def store(lanes, value):
                    SF[q, at, lanes] = value
                split(F[0, f, z + 4, 8 + 16 * q:24 + 16 * q], store)

    ox = lax.rem(offsets_ref[0, me_s], nx)
    oy = lax.rem(offsets_ref[1, me_s], ny)
    lane_shift = lax.rem(ny - oy, ny)
    for k in range(5):
        for j in range(half):
            here = is_self & (j_me == j)
            away = not_self | (j_me != j)
            pl.when(here)(lambda: local(k).wait())
            pl.when(away)(lambda: remote(sendbuf.at[0, k], pin.at[j, k], asend.at[0, k], arecv.at[j, k],
                                         (src_s, src_h * half + j)).wait_recv())

        @pl.loop(0, nz // 2)
        def _(zz):
            for j in range(half):
                two = pin[j, k, pl.ds(pl.multiple_of(zz * 16, 16), 16)].astype(F32)
                for half_row in range(2):
                    part = two[8 * half_row:8 * half_row + 8]
                    dbl[zz * 2 + half_row, 8 * j:8 * j + 8] = part
                    dbl[zz * 2 + half_row, nx + 8 * j:nx + 8 * j + 8] = part

        @pl.loop(0, nz)
        def _(z):
            TRIG[k, z] = pltpu.roll(dbl[z, pl.ds(ox, nx)], lane_shift, 1)

    source = sources_ref[0]
    first_row = me_b * nz

    @pl.loop(0, nz)
    def _(z):
        for t in range(tiles):
            at = pl.ds(16 * t, 16)
            v = TRIG[0, z, at]
            c = v * v
            a = 1.0 + 2.0 * TRIG[1, z, at]
            b = jnp.sqrt(1.0 + 2.0 * TRIG[2, z, at])
            st, ct = sine_cosine(TRIG[3, z, at])
            sa, ca = sine_cosine(TRIG[4, z, at])
            n_z, n_x, n_y = ct, st * ca, st * sa
            TRIG[1, z, at] = st
            TRIG[2, z, at] = ct
            TRIG[3, z, at] = sa
            TRIG[4, z, at] = ca
            mixed = 2.0 * UNIT11 / UNIT2
            COEF[0, z, at] = n_z * n_z
            COEF[1, z, at] = n_x * n_x
            COEF[2, z, at] = mixed * n_z * n_x
            COEF[3, z, at] = mixed * n_z * n_y
            COEF[4, z, at] = mixed * n_x * n_y
            COEF[5, z, at] = a
            COEF[6, z, at] = b
            COEF[7, z, at] = UNIT2 * c
            cell = (((first_row + z) * nx + 16 * t + lax.broadcasted_iota(jnp.int32, (16, ny), 0)) * ny
                    + lax.broadcasted_iota(jnp.int32, (16, ny), 1))
            COEF[8, z, at] = jnp.where(cell == source, c, 0.0)
            for n in range(8):
                ACC[n, z, at] = jnp.zeros((16, ny), F32)

    loads[4].wait()

    def depth_pass(cur, q):
        for f in range(2):
            row = [F[cur, f, z, 8 + 16 * q:24 + 16 * q] for z in range(nz + 8)]
            for z in range(nz):
                ZZ[f, z, 16 * q:16 * q + 16] = second(lambda k: row[z + 4 + k])
                g = first(lambda k: row[z + 4 + k])
                GZ[f, z, 8 + 16 * q:24 + 16 * q] = g
                at = (f * nz + z) * 16

                def store(lanes, value):
                    SG[q, at:at + 16, lanes] = value
                split(g, store)

    def update(t, cur, nxt, q, z, amplitude):
        at = pl.ds(16 * q, 16)
        inner = pl.ds(8 + 16 * q, 16)

        def parts(f):
            def x_of(ref, *lead):
                return lambda k: ref[(*lead, pl.ds(8 + 16 * q + k, 16))]
            yy = YY[f, z, at]
            return (
                ZZ[f, z, at] - yy,
                second(x_of(F, cur, f, z + 4)) - yy,
                first(x_of(GZ, f, z)),
                ZY[q, pl.ds(pl.multiple_of((f * nz + z) * 16, 16), 16)],
                first(x_of(GY, f, z)),
                yy,
                F[cur, f, z + 4, inner],
            )
        coef = [COEF[n, z, at] for n in range(5)]
        dp = parts(0)
        dq = parts(1)

        def weighted(d):
            total = coef[0] * d[0]
            for n in range(1, 5):
                total = total + coef[n] * d[n]
            return total
        base_p = dp[5] + CENTRE * dp[6]
        base_q = dq[5] + CENTRE * dq[6]
        h2 = (dp[0] + dp[1]) + (base_p + base_p) - weighted(dp)
        h1 = base_q + weighted(dq)
        a = COEF[5, z, at]
        b = COEF[6, z, at]
        c = COEF[7, z, at]
        pn = (dp[6] + dp[6]) - F[nxt, 0, z + 4, inner] + c * (a * h2 + b * h1)
        pn = pn + amplitude * COEF[8, z, at]
        qn = (dq[6] + dq[6]) - F[nxt, 1, z + 4, inner] + c * (b * h2 + h1)
        F[nxt, 0, z + 4, inner] = pn
        F[nxt, 1, z + 4, inner] = qn
        for f, value in ((0, pn), (1, qn)):
            def store(lanes, part):
                SF[q, pl.ds(pl.multiple_of((f * nz + z) * 16, 16), 16), lanes] = part
            split(value, store)
        pf = SNAP[t, 0, z, at].astype(F32)
        qf = SNAP[t, 1, z, at].astype(F32)
        bp = b * pf
        wa = a * pf + b * qf
        wb = bp + qf
        ACC[0, z, at] += h2 * wa + h1 * wb
        ACC[1, z, at] += h2 * pf
        ACC[2, z, at] += h1 * pf + h2 * qf
        for n in range(5):
            ACC[3 + n, z, at] += dq[n] * wb - dp[n] * wa

    def step(t, carry):
        cur = lax.rem(t, 2)
        nxt = 1 - cur
        amplitude = traces_ref[0, t]
        for q in range(tiles):
            along_y(q)
        wait_halos(cur, 0)
        depth_pass(cur, 0)
        for q in range(tiles):
            if q + 1 < tiles:
                wait_halos(cur, q + 1)
                depth_pass(cur, q + 1)
            ZY[q] = jnp.dot(SG[q], y1_ref[:, 0:ny], preferred_element_type=F32)
            for direction in range(2):
                for z in range(4):
                    update(t, cur, nxt, q, 8 * direction + z, amplitude)
                pl.when(t < nt - 1)(lambda: send_halos(nxt, q, direction))
        for q in range(tiles):
            @pl.loop(4, 8, step=4)
            def _(z0):
                for z in range(4):
                    update(t, cur, nxt, q, z0 + z, amplitude)
        return carry

    lax.fori_loop(0, nt, step, 0)
    last = nt % 2
    for f in range(2):
        @pl.loop(0, nz)
        def _(z):
            final_ref[f, z] = F[last, f, z + 4, 8:8 + nx]

    back_shift = lax.rem(nx - ox, nx)
    MX[...] = jnp.zeros_like(MX)

    @pl.loop(0, nz)
    def _(z):
        v = TRIG[0, z]
        st, ct, sa, ca = (TRIG[n, z] for n in range(1, 5))
        c = v * v
        b = COEF[6, z]
        n_z, n_x, n_y = ct, st * ca, st * sa
        g = [ACC[n, z] for n in range(8)]
        t_z, t_x, t_y = -st, ct * ca, ct * sa
        a_x, a_y = -st * sa, st * ca
        r = UNIT11 / UNIT2
        tilt = (t_z * n_z * g[3] + t_x * n_x * g[4]
                + r * ((t_z * n_x + t_x * n_z) * g[5] + (t_z * n_y + t_y * n_z) * g[6]
                       + (t_x * n_y + t_y * n_x) * g[7]))
        turn = (a_x * n_x * g[4]
                + r * (a_x * n_z * g[5] + a_y * n_z * g[6] + (a_x * n_y + a_y * n_x) * g[7]))
        sums = (
            2.0 * UNIT2 * v * g[0],
            2.0 * UNIT2 * c * g[1],
            UNIT2 * (c / b) * g[2],
            2.0 * UNIT2 * c * tilt,
            2.0 * UNIT2 * c * turn,
        )
        for k in range(5):
            for part in range(2):
                dbl[k, part * nx:(part + 1) * nx] = sums[k]
        for k in range(5):
            value = pltpu.roll(dbl[k, pl.ds(back_shift, nx)], oy, 1)
            TRIG[k, z] = value
            MX[k] = jnp.maximum(MX[k], jnp.abs(value))

    def exponent_of(largest):
        return jnp.ceil(jnp.log2(jnp.maximum(jnp.max(largest, axis=0, keepdims=True), 1e-30)))

    def exponent_rows(exponents):
        rest = [jnp.zeros_like(exponents[0])] * (EXPONENT_ROWS - len(exponents))
        return jnp.concatenate(exponents + rest, axis=0).astype(jnp.int32).astype(jnp.int16)

    def coded(value):
        return jnp.round(value).astype(jnp.int32).astype(jnp.int16)

    for j in range(half):
        exponents = []
        for k in range(5):
            exponents.append(exponent_of(MX[k, 8 * j:8 * j + 8]))
            MX[k, 8 * j:8 * j + 8] = jnp.broadcast_to(jnp.exp2(14.9 - exponents[k]), (8, ny))
        GQ[j, 0:EXPONENT_ROWS] = exponent_rows(exponents)

    def chunk(n):
        begin = EXPONENT_ROWS + CHUNKS[n][0] * rows if n else 0
        return pl.ds(begin, EXPONENT_ROWS + (CHUNKS[n][-1] + 1) * rows - begin)

    def hop_z(k, i):
        j = lax.rem(j_me + i, half)
        return remote(GQ.at[j, chunk(k)], first_in.at[j_me, chunk(k)], rsend.at[0, k, j], rrecv.at[0, k, j_me],
                      (me_s, y_lo * half + j))

    def own_z(k):
        return pltpu.make_async_copy(GQ.at[j_me, chunk(k)], first_in.at[j_me, chunk(k)], rloc.at[k, 0])

    for n, members in enumerate(CHUNKS):
        for k in members:
            @pl.loop(0, nz // 2)
            def _(zz):
                for j in range(half):
                    scale = MX[k, 8 * j:8 * j + 8]
                    pair = jnp.concatenate([TRIG[k, 2 * zz, 8 * j:8 * j + 8] * scale,
                                            TRIG[k, 2 * zz + 1, 8 * j:8 * j + 8] * scale], axis=0)
                    GQ[j, pl.ds(pl.multiple_of(EXPONENT_ROWS + k * rows + zz * 16, 16), 16)] = coded(pair)
        own_z(n).start()
        for i in range(1, half):
            hop_z(n, i).start()

    def hop_y(k, i):
        j = lax.rem(j_me + i, half)
        z1, z0, c = j // 4, lax.rem(j // 2, 2), lax.rem(j, 2)
        slot = y_me * 2 + z1
        go = remote(first_in.at[j, chunk(k)], second_in.at[slot, chunk(k)], rsend.at[1, k, j], rrecv.at[1, k, slot],
                    (x * 2 + z0, c * half + j_me))
        stay = pltpu.make_async_copy(first_in.at[j, chunk(k)], second_in.at[slot, chunk(k)], rloc.at[k, 1 + z1])
        return (z0 == y_hi) & (c == y_lo), (z0 != y_hi) | (c != y_lo), go, stay

    def forward_y(k):
        for i in range(half):
            j = lax.rem(j_me + i, half)
            if i == 0:
                own_z(k).wait()
            else:
                remote(GQ.at[j, chunk(k)], first_in.at[j, chunk(k)], rsend.at[0, k, j], rrecv.at[0, k, j],
                       (me_s, y_lo * half + j)).wait_recv()
            stays, moves, go, stay = hop_y(k, i)
            pl.when(moves)(go.start)
            pl.when(stays)(stay.start)

    def hop_x(k, i):
        slot = lax.rem(y_me * 2 + i, 8)
        from_hi, from_lo, z1 = slot // 4, lax.rem(slot // 2, 2), lax.rem(slot, 2)
        to_x = 2 * from_lo + z1
        shot = x * 2 + from_hi
        go = remote(second_in.at[slot, chunk(k)], third_in.at[shot, chunk(k)], rsend.at[2, k, slot],
                    rrecv.at[2, k, shot], (to_x * 2 + y_hi, me_b))
        stay = pltpu.make_async_copy(second_in.at[slot, chunk(k)], third_in.at[shot, chunk(k)],
                                     rloc.at[k, 3 + from_hi])
        return to_x == x, to_x != x, go, stay

    def forward_x(k):
        for i in range(8):
            slot = lax.rem(y_me * 2 + i, 8)
            if i < 2:
                pltpu.make_async_copy(first_in.at[0, chunk(k)], second_in.at[slot, chunk(k)], rloc.at[k, 1 + i]).wait()
            else:
                from_hi, from_lo = slot // 4, lax.rem(slot // 2, 2)
                remote(first_in.at[0, chunk(k)], second_in.at[slot, chunk(k)], rsend.at[1, k, 0],
                       rrecv.at[1, k, slot], (x * 2 + from_hi, from_lo * half + j_me)).wait_recv()
            stays, moves, go, stay = hop_x(k, i)
            pl.when(moves)(go.start)
            pl.when(stays)(stay.start)

    def swap(k):
        return remote(swap_out.at[k], swap_in.at[k], ssend.at[k], srecv.at[k], partner)

    def arrive(k):
        for i in range(shots):
            s = lax.rem(me_s + i, shots)
            here = s // 2 == x
            away = s // 2 != x
            pl.when(here)(lambda: pltpu.make_async_copy(
                second_in.at[0, chunk(k)], third_in.at[s, chunk(k)], rloc.at[k, 3 + lax.rem(s, 2)]).wait())
            pl.when(away)(lambda: remote(
                second_in.at[0, chunk(k)], third_in.at[s, chunk(k)], rsend.at[2, k, 0], rrecv.at[2, k, s],
                (s // 2 * 2 + y_hi, me_b)).wait_recv())

    def gather(k):
        scales = []
        for s in range(shots):
            exponents = third_in[s, 0:EXPONENT_ROWS].astype(jnp.int32).astype(F32)
            scales.append(jnp.broadcast_to(jnp.exp2(exponents[k:k + 1] - 14.9), (16, 128)))

        @pl.loop(0, rows // 16)
        def _(r):
            at = pl.ds(pl.multiple_of(r * 16, 16), 16)
            total = [[0.0, 0.0], [0.0, 0.0]]
            for s in range(shots):
                upper = residue < offsets_ref[0, s]
                right = lane < offsets_ref[1, s]
                g = third_in[s, pl.ds(pl.multiple_of(EXPONENT_ROWS + k * rows + r * 16, 16), 16)]
                g = g.astype(jnp.int32).astype(F32) * scales[s]
                hi = jnp.where(upper, g, 0.0)
                for c, part in ((0, g - hi), (1, hi)):
                    right_part = jnp.where(right, part, 0.0)
                    total[c][1] = total[c][1] + right_part
                    total[c][0] = total[c][0] + (part - right_part)
            for c in range(2):
                acc[c, k, at, 0:128] = total[c][0]
                acc[c, k, at, 128:256] = total[c][1]
        largest = jnp.abs(acc[1 - h, k, 0:8])
        for r in range(1, rows // 8):
            largest = jnp.maximum(largest, jnp.abs(acc[1 - h, k, 8 * r:8 * r + 8]))
        exponent = exponent_of(largest)
        swap_out[k, 0:EXPONENT_ROWS] = exponent_rows([exponent])
        scale = jnp.broadcast_to(jnp.exp2(14.9 - exponent), (16, 2 * ny))

        @pl.loop(0, rows // 16)
        def _(r):
            at = pl.ds(pl.multiple_of(r * 16, 16), 16)
            swap_out[k, pl.ds(pl.multiple_of(EXPONENT_ROWS + r * 16, 16), 16)] = coded(acc[1 - h, k, at] * scale)
        swap(k).start()
        out_ref[k, pl.ds(pl.multiple_of(h * rows, 8), rows)] = acc[h, k]

    def finish(k):
        swap(k).wait()
        exponent = swap_in[k, 0:EXPONENT_ROWS].astype(jnp.int32).astype(F32)[0:1]
        scale = jnp.broadcast_to(jnp.exp2(exponent - 14.9), (16, 2 * ny))

        @pl.loop(0, rows // 16)
        def _(r):
            g = swap_in[k, pl.ds(pl.multiple_of(EXPONENT_ROWS + r * 16, 16), 16)].astype(jnp.int32).astype(F32)
            out_ref[k, pl.ds(pl.multiple_of((1 - h) * rows + r * 16, 8), 16)] = g * scale

    for n in range(len(CHUNKS) + 2):
        if n < len(CHUNKS):
            forward_y(n)
        if 1 <= n < len(CHUNKS) + 1:
            forward_x(n - 1)
        if 2 <= n:
            arrive(n - 2)
            for k in CHUNKS[n - 2]:
                gather(k)
    for k in range(5):
        finish(k)

    for k in range(5):
        pl.when(not_self)(lambda: outgoing(0, k).wait_send())
        for i in range(1, shots):
            outgoing(i, k).wait_send()
    for n in range(len(CHUNKS)):
        for i in range(1, half):
            hop_z(n, i).wait_send()
        for i in range(half):
            stays, moves, go, stay = hop_y(n, i)
            pl.when(moves)(go.wait_send)
        for i in range(8):
            stays, moves, go, stay = hop_x(n, i)
            pl.when(moves)(go.wait_send)


def place_kernel(gradients_ref, final_ref, gradients_out, final_out):
    gradients_out[...] = gradients_ref[...]
    final_out[...] = final_ref[...]


def y_matrix(ny):
    matrix = [[0.0] * (2 * ny) for _ in range(ny)]
    for y in range(ny):
        for k in range(1, 5):
            if y + k < ny:
                matrix[y + k][y] = FIRST[k - 1]
                matrix[y + k][ny + y] = SECOND[k - 1]
            if y - k >= 0:
                matrix[y - k][y] = -FIRST[k - 1]
                matrix[y - k][ny + y] = SECOND[k - 1]
    one = jnp.asarray(matrix, F32).astype(BF16)
    return jnp.concatenate([one, one], axis=0)


def on_device(velocity, epsilon, delta, tilt, azimuth, offsets, sources, traces, adjoint_state, snapshots):
    shots = lax.axis_size("shot")
    slabs = lax.axis_size("slab")
    half = slabs // 2
    _, _, nz, nx, ny = adjoint_state.shape
    nt = snapshots.shape[0]
    depth, width, lanes = velocity.shape
    rows = depth * width // 2
    tiles = nx // 16
    vmem = pl.BlockSpec(memory_space=pltpu.VMEM)
    smem = pl.BlockSpec(memory_space=pltpu.SMEM)
    hbm = pl.BlockSpec(memory_space=pl.ANY)
    dma = pltpu.SemaphoreType.DMA
    params = [m.reshape(depth * width, lanes) for m in (velocity, epsilon, delta, tilt, azimuth)]
    state = adjoint_state.reshape(4, nz, nx, ny)
    frames = snapshots.reshape(nt, 2, nz, nx, ny)
    coded = (8, EXPONENT_ROWS + 5 * rows, ny)
    final, gradients = pl.pallas_call(
        whole_kernel,
        out_shape=(
            jax.ShapeDtypeStruct((2, nz, nx, ny), F32),
            jax.ShapeDtypeStruct((5, 2 * rows, lanes), F32),
        ),
        in_specs=[vmem] * 5 + [smem] * 3 + [hbm, hbm, vmem],
        out_specs=(vmem, vmem),
        scratch_shapes=[
            pltpu.VMEM((2, 5, rows, lanes), BF16),
            pltpu.VMEM((shots, 5, rows, ny), BF16),
            pltpu.VMEM((half, 5, rows, ny), BF16),
            pltpu.VMEM((2, 2, nz + 8, nx + 16, ny), F32),
            pltpu.VMEM((2, nz, nx + 16, ny), F32),
            pltpu.VMEM((2, nz, nx + 16, ny), F32),
            pltpu.VMEM((2, nz, nx, ny), F32),
            pltpu.VMEM((2, nz, nx, ny), F32),
            pltpu.VMEM((tiles, 2 * nz * 16, ny), F32),
            pltpu.VMEM((tiles, 2 * nz * 16, 2 * ny), BF16),
            pltpu.VMEM((tiles, 2 * nz * 16, 2 * ny), BF16),
            pltpu.VMEM((9, nz, nx, ny), F32),
            pltpu.VMEM((8, nz, nx, ny), F32),
            pltpu.VMEM((5, nz, nx, ny), F32),
            pltpu.VMEM((nz, 2 * nx, ny), F32),
            pltpu.VMEM((nt, 2, nz, nx, ny), BF16),
            pltpu.VMEM((5, nx, ny), F32),
            pltpu.VMEM(coded, jnp.int16),
            pltpu.VMEM(coded, jnp.int16),
            pltpu.VMEM(coded, jnp.int16),
            pltpu.VMEM(coded, jnp.int16),
            pltpu.VMEM((2, 5, rows, lanes), F32),
            pltpu.VMEM((5, EXPONENT_ROWS + rows, lanes), jnp.int16),
            pltpu.VMEM((5, EXPONENT_ROWS + rows, lanes), jnp.int16),
            dma((5,)), dma((5,)), dma((5,)), dma((shots, 5)), dma((half, 5)), dma((5,)),
            dma((2, 2, tiles)), dma((2, 2, tiles)),
            dma((3, 5, 8)), dma((3, 5, 8)), dma((5, 5)), dma((5,)), dma((5,)),
        ],
        compiler_params=pltpu.CompilerParams(collective_id=0, has_side_effects=True, vmem_limit_bytes=VMEM_LIMIT),
        name="whole",
    )(*params, offsets.T, sources, traces, state, frames, y_matrix(ny))
    gradients, final = pl.pallas_call(
        place_kernel,
        out_shape=(
            jax.ShapeDtypeStruct((5, 2 * rows, lanes), F32),
            jax.ShapeDtypeStruct((2, nz, nx, ny), F32),
        ),
        grid=(2,),
        in_specs=[pl.BlockSpec((5, rows, lanes), lambda i: (0, i, 0)), pl.BlockSpec((1, nz, nx, ny), lambda i: (i, 0, 0, 0))],
        out_specs=(pl.BlockSpec((5, rows, lanes), lambda i: (0, i, 0)), pl.BlockSpec((1, nz, nx, ny), lambda i: (i, 0, 0, 0))),
        compiler_params=pltpu.CompilerParams(vmem_limit_bytes=VMEM_LIMIT),
        name="place",
    )(gradients, final)
    return (gradients.reshape(5, depth, width, lanes), final.reshape(2, 1, nz, nx, ny))


def solution(mesh):
    return jax.shard_map(
        on_device,
        mesh=mesh,
        in_specs=(
            P("shot", "slab", None),
            P("shot", "slab", None),
            P("shot", "slab", None),
            P("shot", "slab", None),
            P("shot", "slab", None),
            P(),
            P("shot"),
            P("shot", None),
            P(None, "shot", "slab", None, None),
            P(None, None, "shot", "slab", None, None),
        ),
        out_specs=(P(None, "shot", "slab", None), P(None, "shot", "slab", None, None)),
        check_vma=False,
    )
```
